32 devices in a mesh: bubble: 8 (over z, y), panel: 4 (over x, core).
Axes of the slice: x: 2, y: 2, z: 4, core: 2. Of those that a mesh axis runs over, the one named last changes fastest.
Arguments:
- density: float32 [64, 12288], P('bubble', 'panel'), may hold values from -6 to 6
- right_side: float32 [64, 12288], P('bubble', 'panel'), may hold values from -6 to 6
- inv_diag: bfloat16 [64, 96, 128, 128], P('bubble', 'panel')
- near_vals: bfloat16 [64, 96, 4, 128, 128], P('bubble', 'panel'), may hold values from -0.25 to 0.25
- near_bubble: int32 [64, 96, 4], P('bubble', 'panel'), may hold values from 0 to 63, as said below
- near_block: int32 [64, 96, 4], P('bubble', 'panel'), may hold values from 0 to 95
- near_count: int32 [64, 96], P('bubble', 'panel'), may hold values from 1 to 4, as said below
- colour: int32 [64], P('bubble'), may hold values from 0 to 1
- moment_map: bfloat16 [64, 16, 12288], P('bubble', None, 'panel'), may hold values from -0.0546875 to 0.0546875
- spread_map: bfloat16 [64, 16, 12288], P('bubble', None, 'panel'), may hold values from -0.1875 to 0.1875
- centres: float32 [3, 64], replicated, may hold values from 0.2 to 6
Outputs:
- relaxed: float32 [64, 12288], P('bubble', 'panel')
The draws below stay inside these ranges and needn't reach their ends.
Inputs may be any that keep to these rules, and one draw needn't show every extreme that they name: `near_bubble`: every slot of bubble b names a bubble within 8 of b. `near_count`: the first row block of every bubble uses all 4 slots.
All inputs are finite; a program needn't handle non-finite values.
Results may differ from the reference program's by a relative error of at most 0.0041.
Values may be sent and summed in bfloat16 or wider, within the bound.
A program may use at most 64 MiB of HBM per device.

```python
import jax
import jax.numpy as jnp
from jax import lax

P_SIZE = 12288
BLK = 128
K = 16
SLOTS = 4
BUB_DEV = 8
BUBBLES = 64
NB = 96


def draw_inv_diag(key, part):
    shape = (BUBBLES, P_SIZE // BLK, BLK, BLK)
    spread = jax.random.normal(key, shape, jnp.float32) * (0.5 / BLK ** 0.5)
    rows = lax_iota_rows(shape)
    return (spread + rows).astype(jnp.bfloat16)


def lax_iota_rows(shape):
    left = jnp.arange(shape[2])[:, None]
    right = jnp.arange(shape[3])[None, :]
    return jnp.broadcast_to((left == right).astype(jnp.float32), shape)


def draw_near_bubble(key, part):
    shape = (BUBBLES, P_SIZE // BLK, SLOTS)
    offsets = jax.random.randint(key, shape, -BUB_DEV, BUB_DEV + 1)
    owners = jnp.arange(BUBBLES, dtype=jnp.int32)[:, None, None]
    return jnp.clip(owners + offsets, 0, BUBBLES - 1).astype(jnp.int32)


def draw_near_count(key, part):
    counts = jax.random.randint(key, (BUBBLES, P_SIZE // BLK), 1, SLOTS + 1)
    return counts.at[:, 0].set(SLOTS).astype(jnp.int32)


def with_ends(array, key, smallest, largest):
    longest = array.shape.index(max(array.shape))
    spots = []
    for shift in (0, 1):
        where = [jax.random.randint(jax.random.fold_in(key, axis), (), 0, length) for axis, length in enumerate(array.shape)]
        where[longest] = (where[longest] + shift) % array.shape[longest]
        spots.append(tuple(where))
    return array.at[spots[0]].set(smallest).at[spots[1]].set(largest)


def shard_levels(own_key, shape, pieces, low, high):
    loudness, own = 1.0, jax.random.fold_in(own_key, 6)
    for position, parts in pieces:
        steps = jnp.exp(jax.random.uniform(jax.random.fold_in(own, position), (parts,), jnp.float32, low / len(pieces), high / len(pieces)))
        loudness = loudness * jnp.repeat(steps, shape[position] // parts).reshape([-1 if axis == position else 1 for axis in range(len(shape))])
    return loudness


def scatter_about(own_key, extent, scale, bound, split=(), kind=jnp.bfloat16):
    gain = shard_levels(own_key, extent, split, -0.22, 0.18) if split else 1.0
    values = jax.random.normal(own_key, extent, jnp.float32) * scale * gain
    return jnp.minimum(jnp.maximum(values, -bound), bound).astype(kind)


def setup_inputs(seed: int = 0) -> dict:
    streams_of = jax.random.split(jax.random.key(seed), 12)
    density = scatter_about(streams_of[0], (BUBBLES, P_SIZE), 1.0, 6.0, ((0, 8), (1, 4)), jnp.float32)
    right_side = scatter_about(streams_of[1], (BUBBLES, P_SIZE), 1.0, 6.0, ((0, 8), (1, 4)), jnp.float32)
    inv_diag = draw_inv_diag(jax.random.fold_in(streams_of[11], 71), 0)
    near_vals = scatter_about(streams_of[3], (BUBBLES, NB, SLOTS, BLK, BLK), (BLK * SLOTS) ** -0.5, 0.25, ((0, 8), (1, 4)))
    near_bubble = draw_near_bubble(jax.random.fold_in(streams_of[11], 71), 0)
    near_block = with_ends(jax.random.randint(streams_of[5], (BUBBLES, NB, SLOTS), 0, NB), jax.random.fold_in(streams_of[5], 1), 0, NB - 1).astype(jnp.int32)
    near_count = draw_near_count(jax.random.fold_in(streams_of[11], 71), 0)
    colour = with_ends(jax.random.randint(streams_of[7], (BUBBLES,), 0, 2), jax.random.fold_in(streams_of[7], 1), 0, 1).astype(jnp.int32)
    moment_map = scatter_about(streams_of[8], (BUBBLES, K, P_SIZE), P_SIZE ** -0.5, 0.0546875, ((0, 8), (2, 4)))
    spread_map = scatter_about(streams_of[9], (BUBBLES, K, P_SIZE), (K * BUBBLES) ** -0.5, 0.1875, ((0, 8), (2, 4)))
    centres = jnp.clip(jax.random.uniform(streams_of[10], (3, BUBBLES), jnp.float32, 0.2, 6.0), 0.2, 6.0)
    return dict(density=density, right_side=right_side, inv_diag=inv_diag, near_vals=near_vals, near_bubble=near_bubble, near_block=near_block, near_count=near_count, colour=colour, moment_map=moment_map, spread_map=spread_map, centres=centres)


def near_field(dens_bf, near_vals, near_bubble, near_block, near_count):
    blocks = dens_bf.reshape(BUBBLES, P_SIZE // BLK, BLK)

    def one_bubble(items):
        block_vals, src_bubble, src_block, counts = items
        sources = blocks[src_bubble, src_block]
        live_slot = jnp.arange(SLOTS)[None, :] < counts[:, None]
        sources = jnp.where(live_slot[:, :, None], sources, jnp.zeros_like(sources))
        return jnp.einsum('rsij,rsj->ri', block_vals.astype(jnp.float32), sources.astype(jnp.float32))
    return lax.map(one_bubble, (near_vals, near_bubble, near_block, near_count))

def far_kernel(centres):
    diff = centres[:, :, None] - centres[:, None, :]
    direct_sq = lax.optimization_barrier(jnp.sum(diff * diff, axis=0))
    mirrored = centres[2][:, None] + centres[2][None, :]
    image_sq = diff[0] * diff[0] + diff[1] * diff[1] + mirrored * mirrored
    kernel = 1.0 / jnp.sqrt(direct_sq + 1.0) + 1.0 / jnp.sqrt(image_sq + 1.0)
    gap = jnp.abs(jnp.arange(BUBBLES)[:, None] - jnp.arange(BUBBLES)[None, :])
    return jnp.where(gap > BUB_DEV, kernel, jnp.zeros_like(kernel))

def reference(density, right_side, inv_diag, near_vals, near_bubble, near_block, near_count, colour, moment_map, spread_map, centres):
    kernel = far_kernel(centres)
    relaxed = density
    for colour_now in range(2):
        dens_bf = relaxed.astype(jnp.bfloat16)
        near = near_field(dens_bf, near_vals, near_bubble, near_block, near_count).reshape(BUBBLES, P_SIZE)
        moments = jnp.einsum('bki,bi->bk', moment_map.astype(jnp.float32), dens_bf.astype(jnp.float32))
        far_coeff = jnp.dot(kernel, moments, precision=lax.Precision.HIGHEST).astype(jnp.bfloat16)
        far = jnp.einsum('bki,bk->bi', spread_map.astype(jnp.float32), far_coeff.astype(jnp.float32))
        remainder = (right_side - near - far).astype(jnp.bfloat16).reshape(BUBBLES, P_SIZE // BLK, BLK)

        def solve_one(items):
            inverse, rest_rows = items
            return jnp.einsum('rij,rj->ri', inverse.astype(jnp.float32), rest_rows.astype(jnp.float32))
        updated = lax.map(solve_one, (inv_diag, remainder)).reshape(BUBBLES, P_SIZE)
        relaxed = jnp.where((colour == colour_now)[:, None], updated, relaxed)
    return relaxed
```

```python
import functools

import jax
import jax.numpy as jnp
from jax import lax
from jax.experimental import pallas as pl
from jax.experimental.pallas import tpu as pltpu
from jax.sharding import PartitionSpec as P

MESH = pl.DeviceIdType.MESH
F32 = jnp.float32
BF16 = jnp.bfloat16


def dot_nt(left, right):
    return lax.dot_general(left, right, (((1,), (1,)), ((), ())), preferred_element_type=F32)


def kernel(
    nbub,
    npan,
    groups,
    dens_ref,
    rhs_ref,
    inv_hbm,
    near_hbm,
    src_bubble_ref,
    src_block_ref,
    count_ref,
    colour_ref,
    mom_hbm,
    spread_hbm,
    centres_ref,
    out_ref,
    near_v,
    inv_v,
    mom_v,
    spread_v,
    hood,
    onehot,
    picked,
    part_mom,
    all_mom,
    green,
    far_v,
    near_sem,
    inv_sem,
    map_sem,
    dens_send,
    dens_recv,
    part_send,
    part_recv,
    mom_send,
    mom_recv,
):
    bub, panels = dens_ref.shape
    rows, slots, blk = near_v.shape[1], near_v.shape[2], near_v.shape[3]
    pairs = rows // 2
    chunk = rows * bub
    moments = mom_v.shape[0] // bub
    lanes = bub * moments
    peers = 3 * npan
    group_pairs = pairs // groups
    me_b, me_p = lax.axis_index("bubble"), lax.axis_index("panel")
    own_slot = npan + me_p

    def rows_of(slot, first, size):
        return pl.ds(pl.multiple_of(slot * chunk + first, 16), size)

    def cols(first, size):
        return pl.ds(pl.multiple_of(first, 128), size)

    def for_peers(do):
        def step(j, carry):
            side, p = j // npan, lax.rem(j, npan)
            other = me_b + side - 1
            ok = (other >= 0) & (other < nbub) & jnp.logical_not((side == 1) & (p == me_p))

            @pl.when(ok)
            def _():
                do(j, side, p, other)

            return carry

        lax.fori_loop(0, peers, step, 0)

    def for_others(count, me, do):
        def step(j, carry):
            @pl.when(j != me)
            def _():
                do(j)

            return carry

        lax.fori_loop(0, count, step, 0)

    barrier = pltpu.get_barrier_semaphore()

    def greet(j, side, p, other):
        pl.semaphore_signal(barrier, inc=1, device_id=(other, p), device_id_type=MESH)

    def greet_bubble(j):
        pl.semaphore_signal(barrier, inc=1, device_id=(j, me_p), device_id_type=MESH)

    for_peers(greet)
    for_others(nbub, me_b, greet_bubble)

    mom_copy = pltpu.make_async_copy(mom_hbm, mom_v, map_sem.at[0])
    spread_copy = pltpu.make_async_copy(spread_hbm, spread_v, map_sem.at[1])
    mom_copy.start()

    def near_copy(q):
        two = pl.ds(2 * q, 2)
        return pltpu.make_async_copy(near_hbm.at[:, two], near_v.at[:, two], near_sem.at[q])

    def inv_copy(q):
        two = pl.ds(2 * q, 2)
        return pltpu.make_async_copy(inv_hbm.at[:, two], inv_v.at[:, two], inv_sem.at[q])

    def start_load(q, carry):
        near_copy(q).start()
        inv_copy(q).start()
        return carry

    lax.fori_loop(0, 1, start_load, 0)
    spread_copy.start()
    lax.fori_loop(1, pairs, start_load, 0)

    def place(q, carry):
        both = jnp.concatenate(
            [dens_ref[:, cols(2 * q * blk, blk)], dens_ref[:, cols((2 * q + 1) * blk, blk)]], axis=0
        )
        hood[0, rows_of(own_slot, q * 16, 16), :] = both.astype(BF16)
        return carry

    lax.fori_loop(0, pairs, place, 0)

    @pl.when(me_b == 0)
    def _():
        hood[:, pl.ds(0, npan * chunk), :] = jnp.zeros((2, npan * chunk, blk), BF16)

    @pl.when(me_b == nbub - 1)
    def _():
        hood[:, pl.ds(2 * npan * chunk, npan * chunk), :] = jnp.zeros((2, npan * chunk, blk), BF16)

    sides = (me_b > 0).astype(jnp.int32) + (me_b < nbub - 1).astype(jnp.int32)
    pl.semaphore_wait(barrier, npan - 1 + npan * sides + nbub - 1)

    def dens_copy(sem, phase, first, size, j, side, p, other):
        piece = hood.at[phase, rows_of(own_slot, first, size)]
        back = (2 - side) * npan + me_p
        return pltpu.make_async_remote_copy(
            src_ref=piece,
            dst_ref=hood.at[phase, rows_of(back, first, size)],
            send_sem=dens_send.at[sem, j],
            recv_sem=dens_recv.at[sem, back],
            device_id=(other, p),
            device_id_type=MESH,
        )

    def dens_arrival(sem, phase, first, size, j, side, p, other):
        piece = hood.at[phase, rows_of(j, first, size)]
        return pltpu.make_async_remote_copy(
            src_ref=piece,
            dst_ref=piece,
            send_sem=dens_send.at[sem, j],
            recv_sem=dens_recv.at[sem, j],
            device_id=(other, p),
            device_id_type=MESH,
        )

    def part_copy(phase, slot, p):
        return pltpu.make_async_remote_copy(
            src_ref=part_mom.at[phase, me_p],
            dst_ref=part_mom.at[phase, slot],
            send_sem=part_send.at[phase, p],
            recv_sem=part_recv.at[phase, slot],
            device_id=(me_b, p),
            device_id_type=MESH,
        )

    def mom_copy_to(phase, slot, b):
        return pltpu.make_async_remote_copy(
            src_ref=all_mom.at[phase, me_b],
            dst_ref=all_mom.at[phase, slot],
            send_sem=mom_send.at[phase, b],
            recv_sem=mom_recv.at[phase, slot],
            device_id=(b, me_p),
            device_id_type=MESH,
        )

    group_rows = group_pairs * 16
    pieces = [(0, 0, 0, chunk)] + [(1 + g, 1, g * group_rows, group_rows) for g in range(groups)]

    for_peers(lambda *a: dens_copy(*pieces[0], *a).start())

    lane = lax.broadcasted_iota(jnp.int32, (bub, lanes), 1)
    row = lax.broadcasted_iota(jnp.int32, (bub, lanes), 0)
    diagonal = lane // moments == row

    def send_moments(phase, source):
        partial = jnp.where(diagonal, dot_nt(source[...].astype(BF16), mom_v[...]), 0.0)
        total = jnp.sum(partial, axis=0, keepdims=True)
        part_mom[phase, me_p] = jnp.broadcast_to(total, (bub, lanes))
        for_others(npan, me_p, lambda p: part_copy(phase, me_p, p).start())

    def pass_moments(phase):
        for_others(npan, me_p, lambda p: part_copy(phase, p, p).wait_recv())
        total = part_mom[phase, 0]
        for p in range(1, npan):
            total = total + part_mom[phase, p]
        all_mom[phase, me_b] = total
        for_others(nbub, me_b, lambda b: mom_copy_to(phase, me_b, b).start())

    def far_field(phase):
        for_others(nbub, me_b, lambda b: mom_copy_to(phase, b, b).wait_recv())
        total = green[0] * all_mom[phase, 0]
        for b in range(1, nbub):
            total = total + green[b] * all_mom[phase, b]
        shift = moments
        while shift < lanes:
            total = total + pltpu.roll(total, shift, 1)
            shift *= 2
        coeff = jnp.where(diagonal, total, 0.0).astype(BF16)
        far_v[...] = jnp.dot(coeff, spread_v[...], preferred_element_type=F32)

    mom_copy.wait()
    send_moments(0, dens_ref)

    def build(b, carry):
        counts = jnp.broadcast_to(count_ref[pl.ds(b, 1), :], (rows, rows))
        on = lax.broadcasted_iota(jnp.int32, (rows, rows), 0) == lax.broadcasted_iota(
            jnp.int32, (rows, rows), 1
        )
        live = jnp.sum(jnp.where(on, counts.astype(F32), 0.0), axis=1, keepdims=True)
        near_bub = src_bubble_ref[b] - (me_b * bub - bub)
        block = src_block_ref[b]
        index = (near_bub // bub * npan + block // rows) * chunk
        index = index + lax.rem(block, rows) * bub + lax.rem(near_bub, bub)
        slot = lax.broadcasted_iota(jnp.int32, (rows, slots), 1).astype(F32)
        index = jnp.where(slot < live, index, -1)
        wide = jnp.concatenate([index[:, s : s + 1] for s in range(slots)], axis=0)
        wide = jnp.broadcast_to(wide, (slots * rows, 128))
        place_of = lax.broadcasted_iota(jnp.int32, (slots * rows, 128), 1)
        for c in range(peers * chunk // 128):
            hit = wide == place_of + c * 128
            onehot[b, :, c * 128 : (c + 1) * 128] = jnp.where(hit, 1.0, 0.0).astype(BF16)
        return carry

    lax.fori_loop(0, bub, build, 0)

    which = lax.broadcasted_iota(jnp.int32, (bub, nbub * bub), 1)
    mine = which == me_b * bub + lax.broadcasted_iota(jnp.int32, (bub, nbub * bub), 0)
    own = [
        jnp.sum(jnp.where(mine, centres_ref[c : c + 1, :], 0.0), axis=1, keepdims=True)
        for c in range(3)
    ]
    spot = lax.broadcasted_iota(jnp.int32, (nbub * bub, lanes), 0)
    over = lax.broadcasted_iota(jnp.int32, (nbub * bub, lanes), 1) // moments
    for b in range(nbub):
        spread_out = jnp.where(spot == over + b * bub, 1.0, 0.0)
        wide = jnp.dot(
            centres_ref[...], spread_out, precision=lax.Precision.HIGHEST, preferred_element_type=F32
        )
        dx, dy, dz = [own[c] - wide[c : c + 1, :] for c in range(3)]
        flat = dx * dx + dy * dy
        up = own[2] + wide[2:3, :]
        value = 1.0 / jnp.sqrt(flat + dz * dz + 1.0) + 1.0 / jnp.sqrt(flat + up * up + 1.0)
        gap = jnp.abs(me_b * bub + row - (b * bub + lane // moments))
        green[b] = jnp.where(gap > bub, value, 0.0)

    tint = jnp.zeros((bub, blk), jnp.int32)
    line = lax.broadcasted_iota(jnp.int32, (bub, blk), 0)
    for b in range(bub):
        tint = jnp.where(line == b, colour_ref[b], tint)

    pass_moments(0)

    def pick(phase):
        def step(b, carry):
            got = jnp.dot(onehot[b], hood[phase], preferred_element_type=F32)
            picked[pl.ds(b, slots * rows, stride=bub), :] = got
            return carry

        lax.fori_loop(0, bub, step, 0)

    def by_bubble(left, right_of):
        even = jnp.zeros((bub, blk), F32)
        odd = jnp.zeros((bub, blk), F32)
        for b in range(bub):
            got = dot_nt(left, right_of(b))
            even = jnp.where(line == b, got[:bub, :blk], even)
            odd = jnp.where(line == b, got[bub:, blk:], odd)
        return jnp.concatenate([even, odd], axis=0)

    def stacked(ref, q):
        first, second = cols(2 * q * blk, blk), cols((2 * q + 1) * blk, blk)
        return jnp.concatenate([ref[:, first], ref[:, second]], axis=0)

    def near_block(b, q):
        return jnp.concatenate(
            [
                jnp.concatenate([near_v[b, 2 * q + o, s] for s in range(slots)], axis=1)
                for o in range(2)
            ],
            axis=0,
        )

    def inv_block(b, q):
        return jnp.concatenate([inv_v[b, 2 * q], inv_v[b, 2 * q + 1]], axis=0)

    def solve(phase, old_ref, q):
        left = jnp.concatenate(
            [
                picked[pl.ds(pl.multiple_of((s * rows + 2 * q) * bub, 16), 16), :].astype(BF16)
                for s in range(slots)
            ],
            axis=1,
        )
        near = by_bubble(left, lambda b: near_block(b, q))
        rest = (stacked(rhs_ref, q) - near - stacked(far_v, q)).astype(BF16)
        updated = by_bubble(rest, lambda b: inv_block(b, q))
        both = jnp.concatenate([tint, tint], axis=0)
        new = jnp.where(both == phase, updated, stacked(old_ref, q))
        out_ref[:, cols(2 * q * blk, blk)] = new[:bub]
        out_ref[:, cols((2 * q + 1) * blk, blk)] = new[bub:]
        return new

    spread_copy.wait()
    far_field(0)
    for_peers(lambda *a: dens_arrival(*pieces[0], *a).wait_recv())
    pick(0)

    def first_colour(q, carry):
        near_copy(q).wait()
        inv_copy(q).wait()
        new = solve(0, dens_ref, q)
        hood[1, rows_of(own_slot, q * 16, 16), :] = new.astype(BF16)
        return carry

    for g in range(groups):
        lax.fori_loop(g * group_pairs, (g + 1) * group_pairs, first_colour, 0)
        for_peers(lambda *a: dens_copy(*pieces[1 + g], *a).start())

    send_moments(1, out_ref)
    pass_moments(1)
    far_field(1)
    for g in range(groups):
        for_peers(lambda *a: dens_arrival(*pieces[1 + g], *a).wait_recv())
    pick(1)

    def second_colour(q, carry):
        solve(1, out_ref, q)
        return carry

    lax.fori_loop(0, pairs, second_colour, 0)

    for piece in pieces:
        for_peers(lambda *a: dens_copy(*piece, *a).wait_send())
    for phase in range(2):
        for_others(npan, me_p, lambda p: part_copy(phase, me_p, p).wait_send())
        for_others(nbub, me_b, lambda b: mom_copy_to(phase, me_b, b).wait_send())


def per_device(
    density,
    right_side,
    inv_diag,
    near_vals,
    near_bubble,
    near_block,
    near_count,
    colour,
    moment_map,
    spread_map,
    centres,
):
    nbub, npan = lax.axis_size("bubble"), lax.axis_size("panel")
    bub, panels = density.shape
    rows, slots, blk = near_vals.shape[1:4]
    moments = moment_map.shape[1]
    lanes = bub * moments
    groups = 3 if (rows // 2) % 3 == 0 else 1
    pairs = rows // 2
    chunk = rows * bub
    hood_rows = 3 * npan * chunk
    vmem = pl.BlockSpec(memory_space=pltpu.VMEM)
    smem = pl.BlockSpec(memory_space=pltpu.SMEM)
    hbm = pl.BlockSpec(memory_space=pl.ANY)
    dma = pltpu.SemaphoreType.DMA
    return pl.pallas_call(
        functools.partial(kernel, nbub, npan, groups),
        out_shape=jax.ShapeDtypeStruct(density.shape, F32),
        in_specs=[vmem, vmem, hbm, hbm, vmem, vmem, vmem, smem, hbm, hbm, vmem],
        out_specs=vmem,
        scratch_shapes=[
            pltpu.VMEM(near_vals.shape, BF16),
            pltpu.VMEM(inv_diag.shape, BF16),
            pltpu.VMEM((lanes, panels), BF16),
            pltpu.VMEM((lanes, panels), BF16),
            pltpu.VMEM((2, hood_rows, blk), BF16),
            pltpu.VMEM((bub, slots * rows, hood_rows), BF16),
            pltpu.VMEM((slots * rows * bub, blk), F32),
            pltpu.VMEM((2, npan, bub, lanes), F32),
            pltpu.VMEM((2, nbub, bub, lanes), F32),
            pltpu.VMEM((nbub, bub, lanes), F32),
            pltpu.VMEM((bub, panels), F32),
            dma((pairs,)),
            dma((pairs,)),
            dma((2,)),
            dma((1 + groups, 3 * npan)),
            dma((1 + groups, 3 * npan)),
            dma((2, npan)),
            dma((2, npan)),
            dma((2, nbub)),
            dma((2, nbub)),
        ],
        compiler_params=pltpu.CompilerParams(
            collective_id=0, has_side_effects=True, vmem_limit_bytes=56 * 1024 * 1024
        ),
    )(
        density,
        right_side,
        inv_diag,
        near_vals,
        near_bubble,
        near_block,
        near_count,
        colour,
        moment_map.reshape(lanes, panels),
        spread_map.reshape(lanes, panels),
        centres,
    )


def solution(mesh):
    in_specs = (
        P("bubble", "panel"),
        P("bubble", "panel"),
        P("bubble", "panel", None, None),
        P("bubble", "panel", None, None, None),
        P("bubble", "panel", None),
        P("bubble", "panel", None),
        P("bubble", "panel"),
        P("bubble"),
        P("bubble", None, "panel"),
        P("bubble", None, "panel"),
        P(),
    )
    out_specs = P("bubble", "panel")
    return jax.shard_map(
        per_device, mesh=mesh, in_specs=in_specs, out_specs=out_specs, check_vma=False
    )
```

```python
import functools

import jax
import jax.numpy as jnp
from jax import lax
from jax.experimental import pallas as pl
from jax.experimental.pallas import tpu as pltpu
from jax.sharding import PartitionSpec as P

MESH = pl.DeviceIdType.MESH
F32 = jnp.float32
BF16 = jnp.bfloat16


def dot_nt(left, right):
    return lax.dot_general(left, right, (((1,), (1,)), ((), ())), preferred_element_type=F32)


def kernel(
    nbub,
    npan,
    groups,
    dens_ref,
    rhs_ref,
    inv_hbm,
    near_hbm,
    src_bubble_ref,
    src_block_ref,
    count_ref,
    colour_ref,
    mom_hbm,
    spread_hbm,
    centres_ref,
    out_ref,
    near_v,
    inv_v,
    mom_v,
    spread_v,
    hood,
    onehot,
    picked,
    part_mom,
    all_mom,
    green,
    far_v,
    near_sem,
    inv_sem,
    map_sem,
    dens_send,
    dens_recv,
    part_send,
    part_recv,
    mom_send,
    mom_recv,
):
    bub, panels = dens_ref.shape
    rows, slots, blk = near_v.shape[1], near_v.shape[2], near_v.shape[3]
    pairs = rows // 2
    chunk = rows * bub
    moments = mom_v.shape[0] // bub
    lanes = bub * moments
    peers = 3 * npan
    group_pairs = pairs // groups
    me_b, me_p = lax.axis_index("bubble"), lax.axis_index("panel")
    own_slot = npan + me_p

    def rows_of(slot, first, size):
        return pl.ds(pl.multiple_of(slot * chunk + first, 16), size)

    def cols(first, size):
        return pl.ds(pl.multiple_of(first, 128), size)

    def for_peers(do):
        def step(j, carry):
            side, p = j // npan, lax.rem(j, npan)
            other = me_b + side - 1
            ok = (other >= 0) & (other < nbub) & jnp.logical_not((side == 1) & (p == me_p))

            @pl.when(ok)
            def _():
                do(j, side, p, other)

            return carry

        lax.fori_loop(0, peers, step, 0)

    def for_others(count, me, do):
        def step(j, carry):
            @pl.when(j != me)
            def _():
                do(j)

            return carry

        lax.fori_loop(0, count, step, 0)

    barrier = pltpu.get_barrier_semaphore()

    def greet(j, side, p, other):
        pl.semaphore_signal(barrier, inc=1, device_id=(other, p), device_id_type=MESH)

    def greet_bubble(j):
        pl.semaphore_signal(barrier, inc=1, device_id=(j, me_p), device_id_type=MESH)

    for_peers(greet)
    for_others(nbub, me_b, greet_bubble)

    mom_copy = pltpu.make_async_copy(mom_hbm, mom_v, map_sem.at[0])
    spread_copy = pltpu.make_async_copy(spread_hbm, spread_v, map_sem.at[1])
    mom_copy.start()

    def near_copy(q):
        two = pl.ds(2 * q, 2)
        return pltpu.make_async_copy(near_hbm.at[:, two], near_v.at[:, two], near_sem.at[q])

    def inv_copy(q):
        two = pl.ds(2 * q, 2)
        return pltpu.make_async_copy(inv_hbm.at[:, two], inv_v.at[:, two], inv_sem.at[q])

    def start_load(q, carry):
        near_copy(q).start()
        inv_copy(q).start()
        return carry

    lax.fori_loop(0, 1, start_load, 0)
    spread_copy.start()
    lax.fori_loop(1, pairs, start_load, 0)

    def place(q, carry):
        both = jnp.concatenate(
            [dens_ref[:, cols(2 * q * blk, blk)], dens_ref[:, cols((2 * q + 1) * blk, blk)]], axis=0
        )
        hood[0, rows_of(own_slot, q * 16, 16), :] = both.astype(BF16)
        return carry

    lax.fori_loop(0, pairs, place, 0)

    @pl.when(me_b == 0)
    def _():
        hood[:, pl.ds(0, npan * chunk), :] = jnp.zeros((2, npan * chunk, blk), BF16)

    @pl.when(me_b == nbub - 1)
    def _():
        hood[:, pl.ds(2 * npan * chunk, npan * chunk), :] = jnp.zeros((2, npan * chunk, blk), BF16)

    sides = (me_b > 0).astype(jnp.int32) + (me_b < nbub - 1).astype(jnp.int32)
    pl.semaphore_wait(barrier, npan - 1 + npan * sides + nbub - 1)

    def dens_copy(sem, phase, first, size, j, side, p, other):
        piece = hood.at[phase, rows_of(own_slot, first, size)]
        back = (2 - side) * npan + me_p
        return pltpu.make_async_remote_copy(
            src_ref=piece,
            dst_ref=hood.at[phase, rows_of(back, first, size)],
            send_sem=dens_send.at[sem, j],
            recv_sem=dens_recv.at[sem, back],
            device_id=(other, p),
            device_id_type=MESH,
        )

    def dens_arrival(sem, phase, first, size, j, side, p, other):
        piece = hood.at[phase, rows_of(j, first, size)]
        return pltpu.make_async_remote_copy(
            src_ref=piece,
            dst_ref=piece,
            send_sem=dens_send.at[sem, j],
            recv_sem=dens_recv.at[sem, j],
            device_id=(other, p),
            device_id_type=MESH,
        )

    def part_copy(phase, slot, p):
        return pltpu.make_async_remote_copy(
            src_ref=part_mom.at[phase, me_p],
            dst_ref=part_mom.at[phase, slot],
            send_sem=part_send.at[phase, p],
            recv_sem=part_recv.at[phase, slot],
            device_id=(me_b, p),
            device_id_type=MESH,
        )

    def mom_copy_to(phase, slot, b):
        return pltpu.make_async_remote_copy(
            src_ref=all_mom.at[phase, me_b],
            dst_ref=all_mom.at[phase, slot],
            send_sem=mom_send.at[phase, b],
            recv_sem=mom_recv.at[phase, slot],
            device_id=(b, me_p),
            device_id_type=MESH,
        )

    group_rows = group_pairs * 16
    pieces = [(0, 0, 0, chunk)] + [(1 + g, 1, g * group_rows, group_rows) for g in range(groups)]

    for_peers(lambda *a: dens_copy(*pieces[0], *a).start())

    lane = lax.broadcasted_iota(jnp.int32, (bub, lanes), 1)
    row = lax.broadcasted_iota(jnp.int32, (bub, lanes), 0)
    diagonal = lane // moments == row

    def send_moments(phase, source):
        partial = jnp.where(diagonal, dot_nt(source[...].astype(BF16), mom_v[...]), 0.0)
        total = jnp.sum(partial, axis=0, keepdims=True)
        part_mom[phase, me_p] = jnp.broadcast_to(total, (bub, lanes))
        for_others(npan, me_p, lambda p: part_copy(phase, me_p, p).start())

    def pass_moments(phase):
        for_others(npan, me_p, lambda p: part_copy(phase, p, p).wait_recv())
        total = part_mom[phase, 0]
        for p in range(1, npan):
            total = total + part_mom[phase, p]
        all_mom[phase, me_b] = total
        for_others(nbub, me_b, lambda b: mom_copy_to(phase, me_b, b).start())

    def far_field(phase):
        for_others(nbub, me_b, lambda b: mom_copy_to(phase, b, b).wait_recv())
        total = green[0] * all_mom[phase, 0]
        for b in range(1, nbub):
            total = total + green[b] * all_mom[phase, b]
        shift = moments
        while shift < lanes:
            total = total + pltpu.roll(total, shift, 1)
            shift *= 2
        coeff = jnp.where(diagonal, total, 0.0).astype(BF16)
        far_v[...] = jnp.dot(coeff, spread_v[...], preferred_element_type=F32)

    mom_copy.wait()
    send_moments(0, dens_ref)

    def build(b, carry):
        on = lax.broadcasted_iota(jnp.int32, (rows, rows), 0) == lax.broadcasted_iota(
            jnp.int32, (rows, rows), 1
        )
        near_bub = src_bubble_ref[b] - (me_b * bub - bub)
        block = src_block_ref[b]
        index = (near_bub // bub * npan + block // rows) * chunk
        index = index + lax.rem(block, rows) * bub + lax.rem(near_bub, bub)
        slot = lax.broadcasted_iota(jnp.int32, (slots, rows), 0)
        index = jnp.where(slot < count_ref[pl.ds(b, 1), :], index, -1).astype(F32)
        wide = jnp.concatenate(
            [
                jnp.sum(
                    jnp.where(on, jnp.broadcast_to(index[s : s + 1, :], (rows, rows)), 0.0),
                    axis=1,
                    keepdims=True,
                )
                for s in range(slots)
            ],
            axis=0,
        )
        wide = jnp.broadcast_to(wide, (slots * rows, 128))
        place_of = lax.broadcasted_iota(jnp.int32, (slots * rows, 128), 1).astype(F32)
        mine_rows = pl.ds(pl.multiple_of(b * slots * rows, 16), slots * rows)
        for c in range(peers * chunk // 128):
            hit = wide == place_of + float(c * 128)
            onehot[mine_rows, c * 128 : (c + 1) * 128] = jnp.where(hit, 1.0, 0.0).astype(BF16)
        return carry

    lax.fori_loop(0, bub, build, 0)

    which = lax.broadcasted_iota(jnp.int32, (bub, nbub * bub), 1)
    mine = which == me_b * bub + lax.broadcasted_iota(jnp.int32, (bub, nbub * bub), 0)
    own = [
        jnp.sum(jnp.where(mine, centres_ref[c : c + 1, :], 0.0), axis=1, keepdims=True)
        for c in range(3)
    ]
    spot = lax.broadcasted_iota(jnp.int32, (nbub * bub, lanes), 0)
    over = lax.broadcasted_iota(jnp.int32, (nbub * bub, lanes), 1) // moments
    for b in range(nbub):
        spread_out = jnp.where(spot == over + b * bub, 1.0, 0.0)
        wide = jnp.dot(
            centres_ref[...], spread_out, precision=lax.Precision.HIGHEST, preferred_element_type=F32
        )
        dx, dy, dz = [own[c] - wide[c : c + 1, :] for c in range(3)]
        flat = dx * dx + dy * dy
        up = own[2] + wide[2:3, :]
        value = 1.0 / jnp.sqrt(flat + dz * dz + 1.0) + 1.0 / jnp.sqrt(flat + up * up + 1.0)
        gap = jnp.abs(me_b * bub + row - (b * bub + lane // moments))
        green[b] = jnp.where(gap > bub, value, 0.0)

    tint = jnp.zeros((bub, blk), jnp.int32)
    line = lax.broadcasted_iota(jnp.int32, (bub, blk), 0)
    for b in range(bub):
        tint = jnp.where(line == b, colour_ref[b], tint)

    pass_moments(0)

    def pick(phase):
        size = slots * rows
        half = bub // 2

        def step(h, carry):
            some = onehot[pl.ds(pl.multiple_of(h * half * size, 16), half * size), :]
            got = jnp.dot(some, hood[phase], preferred_element_type=F32)
            for o in range(half):
                picked[pl.ds(h * half + o, size, stride=bub), :] = got[o * size : (o + 1) * size]
            return carry

        lax.fori_loop(0, 2, step, 0)

    def by_bubble(left, right_of):
        even = jnp.zeros((bub, blk), F32)
        odd = jnp.zeros((bub, blk), F32)
        for b in range(bub):
            got = dot_nt(left, right_of(b))
            even = jnp.where(line == b, got[:bub, :blk], even)
            odd = jnp.where(line == b, got[bub:, blk:], odd)
        return jnp.concatenate([even, odd], axis=0)

    def stacked(ref, q):
        first, second = cols(2 * q * blk, blk), cols((2 * q + 1) * blk, blk)
        return jnp.concatenate([ref[:, first], ref[:, second]], axis=0)

    def near_block(b, q):
        return jnp.concatenate(
            [
                jnp.concatenate([near_v[b, 2 * q + o, s] for s in range(slots)], axis=1)
                for o in range(2)
            ],
            axis=0,
        )

    def inv_block(b, q):
        return jnp.concatenate([inv_v[b, 2 * q], inv_v[b, 2 * q + 1]], axis=0)

    both_tint = jnp.concatenate([tint, tint], axis=0)

    def solve(phase, old_ref, some):
        rests = []
        for q in some:
            left = jnp.concatenate(
                [
                    picked[pl.ds(pl.multiple_of((s * rows + 2 * q) * bub, 16), 16), :].astype(BF16)
                    for s in range(slots)
                ],
                axis=1,
            )
            near = by_bubble(left, lambda b: near_block(b, q))
            rests.append((stacked(rhs_ref, q) - near - stacked(far_v, q)).astype(BF16))
        news = []
        for q, rest in zip(some, rests):
            updated = by_bubble(rest, lambda b: inv_block(b, q))
            news.append(jnp.where(both_tint == phase, updated, stacked(old_ref, q)))
        for q, new in zip(some, news):
            out_ref[:, cols(2 * q * blk, blk)] = new[:bub]
            out_ref[:, cols((2 * q + 1) * blk, blk)] = new[bub:]
        return news

    spread_copy.wait()
    for_peers(lambda *a: dens_arrival(*pieces[0], *a).wait_recv())
    pick(0)
    far_field(0)
    batch = 2 if group_pairs % 2 == 0 else 1

    def first_colour(t, carry):
        some = [batch * t + o for o in range(batch)]
        for q in some:
            near_copy(q).wait()
            inv_copy(q).wait()
        for q, new in zip(some, solve(0, dens_ref, some)):
            hood[1, rows_of(own_slot, q * 16, 16), :] = new.astype(BF16)
        return carry

    steps = group_pairs // batch
    for g in range(groups):
        lax.fori_loop(g * steps, (g + 1) * steps, first_colour, 0)
        for_peers(lambda *a: dens_copy(*pieces[1 + g], *a).start())

    send_moments(1, out_ref)
    pass_moments(1)
    for g in range(groups):
        for_peers(lambda *a: dens_arrival(*pieces[1 + g], *a).wait_recv())
    pick(1)
    far_field(1)

    def second_colour(t, carry):
        solve(1, out_ref, [batch * t + o for o in range(batch)])
        return carry

    lax.fori_loop(0, pairs // batch, second_colour, 0)

    for piece in pieces:
        for_peers(lambda *a: dens_copy(*piece, *a).wait_send())
    for phase in range(2):
        for_others(npan, me_p, lambda p: part_copy(phase, me_p, p).wait_send())
        for_others(nbub, me_b, lambda b: mom_copy_to(phase, me_b, b).wait_send())


def per_device(
    density,
    right_side,
    inv_diag,
    near_vals,
    near_bubble,
    near_block,
    near_count,
    colour,
    moment_map,
    spread_map,
    centres,
):
    nbub, npan = lax.axis_size("bubble"), lax.axis_size("panel")
    bub, panels = density.shape
    rows, slots, blk = near_vals.shape[1:4]
    moments = moment_map.shape[1]
    lanes = bub * moments
    groups = 3 if (rows // 2) % 3 == 0 else 1
    pairs = rows // 2
    chunk = rows * bub
    hood_rows = 3 * npan * chunk
    vmem = pl.BlockSpec(memory_space=pltpu.VMEM)
    smem = pl.BlockSpec(memory_space=pltpu.SMEM)
    hbm = pl.BlockSpec(memory_space=pl.ANY)
    dma = pltpu.SemaphoreType.DMA
    return pl.pallas_call(
        functools.partial(kernel, nbub, npan, groups),
        out_shape=jax.ShapeDtypeStruct(density.shape, F32),
        in_specs=[vmem, vmem, hbm, hbm, vmem, vmem, vmem, smem, hbm, hbm, vmem],
        out_specs=vmem,
        scratch_shapes=[
            pltpu.VMEM(near_vals.shape, BF16),
            pltpu.VMEM(inv_diag.shape, BF16),
            pltpu.VMEM((lanes, panels), BF16),
            pltpu.VMEM((lanes, panels), BF16),
            pltpu.VMEM((2, hood_rows, blk), BF16),
            pltpu.VMEM((bub * slots * rows, hood_rows), BF16),
            pltpu.VMEM((slots * rows * bub, blk), F32),
            pltpu.VMEM((2, npan, bub, lanes), F32),
            pltpu.VMEM((2, nbub, bub, lanes), F32),
            pltpu.VMEM((nbub, bub, lanes), F32),
            pltpu.VMEM((bub, panels), F32),
            dma((pairs,)),
            dma((pairs,)),
            dma((2,)),
            dma((1 + groups, 3 * npan)),
            dma((1 + groups, 3 * npan)),
            dma((2, npan)),
            dma((2, npan)),
            dma((2, nbub)),
            dma((2, nbub)),
        ],
        compiler_params=pltpu.CompilerParams(
            collective_id=0, has_side_effects=True, vmem_limit_bytes=56 * 1024 * 1024
        ),
    )(
        density,
        right_side,
        inv_diag,
        near_vals,
        near_bubble.transpose(0, 2, 1),
        near_block.transpose(0, 2, 1),
        near_count,
        colour,
        moment_map.reshape(lanes, panels),
        spread_map.reshape(lanes, panels),
        centres,
    )


def solution(mesh):
    in_specs = (
        P("bubble", "panel"),
        P("bubble", "panel"),
        P("bubble", "panel", None, None),
        P("bubble", "panel", None, None, None),
        P("bubble", "panel", None),
        P("bubble", "panel", None),
        P("bubble", "panel"),
        P("bubble"),
        P("bubble", None, "panel"),
        P("bubble", None, "panel"),
        P(),
    )
    out_specs = P("bubble", "panel")
    return jax.shard_map(
        per_device, mesh=mesh, in_specs=in_specs, out_specs=out_specs, check_vma=False
    )
```

```python
import functools

import jax
import jax.numpy as jnp
from jax import lax
from jax.experimental import pallas as pl
from jax.experimental.pallas import tpu as pltpu
from jax.sharding import PartitionSpec as P

MESH = pl.DeviceIdType.MESH
F32 = jnp.float32
BF16 = jnp.bfloat16


def dot_nt(left, right):
    return lax.dot_general(left, right, (((1,), (1,)), ((), ())), preferred_element_type=F32)


def kernel(
    nbub,
    npan,
    groups,
    dens_ref,
    rhs_ref,
    inv_hbm,
    near_hbm,
    src_bubble_ref,
    src_block_ref,
    count_ref,
    colour_ref,
    mom_hbm,
    spread_hbm,
    centres_ref,
    out_ref,
    near_v,
    inv_v,
    mom_v,
    spread_v,
    hood,
    onehot,
    picked,
    part_mom,
    all_mom,
    green,
    far_v,
    near_sem,
    inv_sem,
    map_sem,
    dens_send,
    dens_recv,
    part_send,
    part_recv,
    mom_send,
    mom_recv,
):
    bub, panels = dens_ref.shape
    rows, slots, blk = near_v.shape[1], near_v.shape[2], near_v.shape[3]
    pairs = rows // 2
    chunk = rows * bub
    moments = mom_v.shape[0] // bub
    lanes = bub * moments
    peers = 3 * npan
    group_pairs = pairs // groups
    me_b, me_p = lax.axis_index("bubble"), lax.axis_index("panel")
    own_slot = npan + me_p

    def rows_of(slot, first, size):
        return pl.ds(pl.multiple_of(slot * chunk + first, 16), size)

    def cols(first, size):
        return pl.ds(pl.multiple_of(first, 128), size)

    def for_peers(do):
        def step(j, carry):
            side, p = j // npan, lax.rem(j, npan)
            other = me_b + side - 1
            ok = (other >= 0) & (other < nbub) & jnp.logical_not((side == 1) & (p == me_p))

            @pl.when(ok)
            def _():
                do(j, side, p, other)

            return carry

        lax.fori_loop(0, peers, step, 0)

    def for_others(count, me, do):
        def step(j, carry):
            @pl.when(j != me)
            def _():
                do(j)

            return carry

        lax.fori_loop(0, count, step, 0)

    barrier = pltpu.get_barrier_semaphore()

    def greet(j, side, p, other):
        pl.semaphore_signal(barrier, inc=1, device_id=(other, p), device_id_type=MESH)

    def greet_bubble(j):
        pl.semaphore_signal(barrier, inc=1, device_id=(j, me_p), device_id_type=MESH)

    for_peers(greet)
    for_others(nbub, me_b, greet_bubble)

    mom_copy = pltpu.make_async_copy(mom_hbm, mom_v, map_sem.at[0])
    spread_copy = pltpu.make_async_copy(spread_hbm, spread_v, map_sem.at[1])
    mom_copy.start()

    def near_copy(q):
        two = pl.ds(2 * q, 2)
        return pltpu.make_async_copy(near_hbm.at[:, two], near_v.at[:, two], near_sem.at[q])

    def inv_copy(q):
        two = pl.ds(2 * q, 2)
        return pltpu.make_async_copy(inv_hbm.at[:, two], inv_v.at[:, two], inv_sem.at[q])

    def start_load(q, carry):
        near_copy(q).start()
        inv_copy(q).start()
        return carry

    lax.fori_loop(0, 1, start_load, 0)
    spread_copy.start()
    lax.fori_loop(1, pairs, start_load, 0)

    def place(q, carry):
        both = jnp.concatenate(
            [dens_ref[:, cols(2 * q * blk, blk)], dens_ref[:, cols((2 * q + 1) * blk, blk)]], axis=0
        )
        hood[0, rows_of(own_slot, q * 16, 16), :] = both.astype(BF16)
        return carry

    lax.fori_loop(0, pairs, place, 0)

    @pl.when(me_b == 0)
    def _():
        hood[:, pl.ds(0, npan * chunk), :] = jnp.zeros((2, npan * chunk, blk), BF16)

    @pl.when(me_b == nbub - 1)
    def _():
        hood[:, pl.ds(2 * npan * chunk, npan * chunk), :] = jnp.zeros((2, npan * chunk, blk), BF16)

    sides = (me_b > 0).astype(jnp.int32) + (me_b < nbub - 1).astype(jnp.int32)
    pl.semaphore_wait(barrier, npan - 1 + npan * sides + nbub - 1)

    def dens_copy(sem, phase, first, size, j, side, p, other):
        piece = hood.at[phase, rows_of(own_slot, first, size)]
        back = (2 - side) * npan + me_p
        return pltpu.make_async_remote_copy(
            src_ref=piece,
            dst_ref=hood.at[phase, rows_of(back, first, size)],
            send_sem=dens_send.at[sem, j],
            recv_sem=dens_recv.at[sem, back],
            device_id=(other, p),
            device_id_type=MESH,
        )

    def dens_arrival(sem, phase, first, size, j, side, p, other):
        piece = hood.at[phase, rows_of(j, first, size)]
        return pltpu.make_async_remote_copy(
            src_ref=piece,
            dst_ref=piece,
            send_sem=dens_send.at[sem, j],
            recv_sem=dens_recv.at[sem, j],
            device_id=(other, p),
            device_id_type=MESH,
        )

    def part_copy(phase, slot, p):
        return pltpu.make_async_remote_copy(
            src_ref=part_mom.at[phase, me_p],
            dst_ref=part_mom.at[phase, slot],
            send_sem=part_send.at[phase, p],
            recv_sem=part_recv.at[phase, slot],
            device_id=(me_b, p),
            device_id_type=MESH,
        )

    def mom_copy_to(phase, slot, b):
        return pltpu.make_async_remote_copy(
            src_ref=all_mom.at[phase, me_b],
            dst_ref=all_mom.at[phase, slot],
            send_sem=mom_send.at[phase, b],
            recv_sem=mom_recv.at[phase, slot],
            device_id=(b, me_p),
            device_id_type=MESH,
        )

    group_rows = group_pairs * 16
    pieces = [(0, 0, 0, chunk)] + [(1 + g, 1, g * group_rows, group_rows) for g in range(groups)]

    for_peers(lambda *a: dens_copy(*pieces[0], *a).start())

    lane = lax.broadcasted_iota(jnp.int32, (bub, lanes), 1)
    row = lax.broadcasted_iota(jnp.int32, (bub, lanes), 0)
    diagonal = lane // moments == row

    def send_moments(phase, source):
        partial = jnp.where(diagonal, dot_nt(source[...].astype(BF16), mom_v[...]), 0.0)
        total = jnp.sum(partial, axis=0, keepdims=True)
        part_mom[phase, me_p] = jnp.broadcast_to(total, (bub, lanes))
        for_others(npan, me_p, lambda p: part_copy(phase, me_p, p).start())

    def pass_moments(phase):
        for_others(npan, me_p, lambda p: part_copy(phase, p, p).wait_recv())
        total = part_mom[phase, 0]
        for p in range(1, npan):
            total = total + part_mom[phase, p]
        all_mom[phase, me_b] = total
        for_others(nbub, me_b, lambda b: mom_copy_to(phase, me_b, b).start())

    def far_field(phase):
        for_others(nbub, me_b, lambda b: mom_copy_to(phase, b, b).wait_recv())
        total = green[0] * all_mom[phase, 0]
        for b in range(1, nbub):
            total = total + green[b] * all_mom[phase, b]
        shift = moments
        while shift < lanes:
            total = total + pltpu.roll(total, shift, 1)
            shift *= 2
        coeff = jnp.where(diagonal, total, 0.0).astype(BF16)
        far_v[...] = jnp.dot(coeff, spread_v[...], preferred_element_type=F32)

    mom_copy.wait()
    send_moments(0, dens_ref)

    def build(b, carry):
        on = lax.broadcasted_iota(jnp.int32, (rows, rows), 0) == lax.broadcasted_iota(
            jnp.int32, (rows, rows), 1
        )
        near_bub = src_bubble_ref[b] - (me_b * bub - bub)
        block = src_block_ref[b]
        index = (near_bub // bub * npan + block // rows) * chunk
        index = index + lax.rem(block, rows) * bub + lax.rem(near_bub, bub)
        slot = lax.broadcasted_iota(jnp.int32, (slots, rows), 0)
        index = jnp.where(slot < count_ref[pl.ds(b, 1), :], index, -1).astype(F32)
        wide = jnp.concatenate(
            [
                jnp.sum(
                    jnp.where(on, jnp.broadcast_to(index[s : s + 1, :], (rows, rows)), 0.0),
                    axis=1,
                    keepdims=True,
                )
                for s in range(slots)
            ],
            axis=0,
        )
        wide = jnp.broadcast_to(wide, (slots * rows, 128))
        place_of = lax.broadcasted_iota(jnp.int32, (slots * rows, 128), 1).astype(F32)
        mine_rows = pl.ds(pl.multiple_of(b * slots * rows, 16), slots * rows)
        for c in range(peers * chunk // 128):
            hit = wide == place_of + float(c * 128)
            onehot[mine_rows, c * 128 : (c + 1) * 128] = jnp.where(hit, 1.0, 0.0).astype(BF16)
        return carry

    lax.fori_loop(0, bub, build, 0)

    which = lax.broadcasted_iota(jnp.int32, (bub, nbub * bub), 1)
    mine = which == me_b * bub + lax.broadcasted_iota(jnp.int32, (bub, nbub * bub), 0)
    own = [
        jnp.sum(jnp.where(mine, centres_ref[c : c + 1, :], 0.0), axis=1, keepdims=True)
        for c in range(3)
    ]
    spot = lax.broadcasted_iota(jnp.int32, (nbub * bub, lanes), 0)
    over = lax.broadcasted_iota(jnp.int32, (nbub * bub, lanes), 1) // moments
    for b in range(nbub):
        spread_out = jnp.where(spot == over + b * bub, 1.0, 0.0)
        wide = jnp.dot(
            centres_ref[...], spread_out, precision=lax.Precision.HIGHEST, preferred_element_type=F32
        )
        dx, dy, dz = [own[c] - wide[c : c + 1, :] for c in range(3)]
        flat = dx * dx + dy * dy
        up = own[2] + wide[2:3, :]
        value = 1.0 / jnp.sqrt(flat + dz * dz + 1.0) + 1.0 / jnp.sqrt(flat + up * up + 1.0)
        gap = jnp.abs(me_b * bub + row - (b * bub + lane // moments))
        green[b] = jnp.where(gap > bub, value, 0.0)

    tint = jnp.zeros((bub, blk), jnp.int32)
    line = lax.broadcasted_iota(jnp.int32, (bub, blk), 0)
    for b in range(bub):
        tint = jnp.where(line == b, colour_ref[b], tint)

    pass_moments(0)

    def pick(phase):
        size = slots * rows
        half = bub // 2

        def step(h, carry):
            some = onehot[pl.ds(pl.multiple_of(h * half * size, 16), half * size), :]
            got = jnp.dot(some, hood[phase], preferred_element_type=F32)
            for o in range(half):
                picked[pl.ds(h * half + o, size, stride=bub), :] = got[o * size : (o + 1) * size]
            return carry

        lax.fori_loop(0, 2, step, 0)

    group_blocks = 2 * group_pairs
    filled = group_blocks * bub
    column = lax.broadcasted_iota(jnp.int32, (blk, blk), 1)
    member = lax.broadcasted_iota(jnp.int32, (filled, blk), 0) // bub

    def group_of(ref, g):
        return jnp.concatenate(
            [ref[:, pl.ds((g * group_blocks + r) * blk, blk)] for r in range(group_blocks)], axis=0
        )

    def filled_out(held):
        if filled == blk:
            return held
        return jnp.concatenate([held, jnp.zeros((blk - filled, held.shape[1]), F32)], axis=0)

    def take(total, got, wanted):
        for b in range(bub):
            hit = wanted(b)
            total = jnp.where(hit, got[b * blk : (b + 1) * blk], total)
        return total

    def solve(phase, old_ref, g):
        first = g * group_blocks
        held = jnp.concatenate(
            [picked[pl.ds((s * rows + first) * bub, filled), :] for s in range(slots)], axis=1
        )
        held = filled_out(held).astype(BF16)

        def near_step(t, total):
            q = g * group_pairs + t
            if phase == 0:
                near_copy(q).wait()
            for o in range(2):
                r = 2 * q + o
                blocks = jnp.concatenate(
                    [near_v[:, r, s].reshape(bub * blk, blk) for s in range(slots)], axis=1
                )
                base = (2 * t + o) * bub
                total = take(total, dot_nt(blocks, held), lambda b: column == base + b)
            return total

        near = lax.fori_loop(0, group_pairs, near_step, jnp.zeros((blk, blk), F32))
        near = near.T[:filled]
        rest = group_of(rhs_ref, g) - near - group_of(far_v, g)

        def solve_step(t, total):
            q = g * group_pairs + t
            if phase == 0:
                inv_copy(q).wait()
            blocks = jnp.concatenate(
                [inv_v[:, 2 * q + o].reshape(bub * blk, blk) for o in range(2)], axis=1
            )
            two = jnp.concatenate(
                [jnp.where(member == 2 * t + o, rest, 0.0) for o in range(2)], axis=1
            )
            got = dot_nt(blocks, filled_out(two).astype(BF16))
            base = 2 * t * bub
            return take(
                total, got, lambda b: (column == base + b) | (column == base + bub + b)
            )

        updated = lax.fori_loop(0, group_pairs, solve_step, jnp.zeros((blk, blk), F32))
        updated = updated.T[:filled]
        tints = jnp.concatenate([tint] * group_blocks, axis=0)
        new = jnp.where(tints == phase, updated, group_of(old_ref, g))
        for r in range(group_blocks):
            out_ref[:, (first + r) * blk : (first + r + 1) * blk] = new[r * bub : (r + 1) * bub]
        return new

    spread_copy.wait()
    for_peers(lambda *a: dens_arrival(*pieces[0], *a).wait_recv())
    pick(0)
    far_field(0)
    for g in range(groups):
        new = solve(0, dens_ref, g)
        hood[1, rows_of(own_slot, g * group_rows, group_rows), :] = new.astype(BF16)
        for_peers(lambda *a: dens_copy(*pieces[1 + g], *a).start())

    send_moments(1, out_ref)
    pass_moments(1)
    for g in range(groups):
        for_peers(lambda *a: dens_arrival(*pieces[1 + g], *a).wait_recv())
    pick(1)
    far_field(1)

    for g in range(groups):
        solve(1, out_ref, g)

    for piece in pieces:
        for_peers(lambda *a: dens_copy(*piece, *a).wait_send())
    for phase in range(2):
        for_others(npan, me_p, lambda p: part_copy(phase, me_p, p).wait_send())
        for_others(nbub, me_b, lambda b: mom_copy_to(phase, me_b, b).wait_send())


def per_device(
    density,
    right_side,
    inv_diag,
    near_vals,
    near_bubble,
    near_block,
    near_count,
    colour,
    moment_map,
    spread_map,
    centres,
):
    nbub, npan = lax.axis_size("bubble"), lax.axis_size("panel")
    bub, panels = density.shape
    rows, slots, blk = near_vals.shape[1:4]
    moments = moment_map.shape[1]
    lanes = bub * moments
    groups = 3 if (rows // 2) % 3 == 0 else 1
    pairs = rows // 2
    chunk = rows * bub
    hood_rows = 3 * npan * chunk
    vmem = pl.BlockSpec(memory_space=pltpu.VMEM)
    smem = pl.BlockSpec(memory_space=pltpu.SMEM)
    hbm = pl.BlockSpec(memory_space=pl.ANY)
    dma = pltpu.SemaphoreType.DMA
    return pl.pallas_call(
        functools.partial(kernel, nbub, npan, groups),
        out_shape=jax.ShapeDtypeStruct(density.shape, F32),
        in_specs=[vmem, vmem, hbm, hbm, vmem, vmem, vmem, smem, hbm, hbm, vmem],
        out_specs=vmem,
        scratch_shapes=[
            pltpu.VMEM(near_vals.shape, BF16),
            pltpu.VMEM(inv_diag.shape, BF16),
            pltpu.VMEM((lanes, panels), BF16),
            pltpu.VMEM((lanes, panels), BF16),
            pltpu.VMEM((2, hood_rows, blk), BF16),
            pltpu.VMEM((bub * slots * rows, hood_rows), BF16),
            pltpu.VMEM((slots * rows * bub, blk), F32),
            pltpu.VMEM((2, npan, bub, lanes), F32),
            pltpu.VMEM((2, nbub, bub, lanes), F32),
            pltpu.VMEM((nbub, bub, lanes), F32),
            pltpu.VMEM((bub, panels), F32),
            dma((pairs,)),
            dma((pairs,)),
            dma((2,)),
            dma((1 + groups, 3 * npan)),
            dma((1 + groups, 3 * npan)),
            dma((2, npan)),
            dma((2, npan)),
            dma((2, nbub)),
            dma((2, nbub)),
        ],
        compiler_params=pltpu.CompilerParams(
            collective_id=0, has_side_effects=True, vmem_limit_bytes=56 * 1024 * 1024
        ),
    )(
        density,
        right_side,
        inv_diag,
        near_vals,
        near_bubble.transpose(0, 2, 1),
        near_block.transpose(0, 2, 1),
        near_count,
        colour,
        moment_map.reshape(lanes, panels),
        spread_map.reshape(lanes, panels),
        centres,
    )


def solution(mesh):
    in_specs = (
        P("bubble", "panel"),
        P("bubble", "panel"),
        P("bubble", "panel", None, None),
        P("bubble", "panel", None, None, None),
        P("bubble", "panel", None),
        P("bubble", "panel", None),
        P("bubble", "panel"),
        P("bubble"),
        P("bubble", None, "panel"),
        P("bubble", None, "panel"),
        P(),
    )
    out_specs = P("bubble", "panel")
    return jax.shard_map(
        per_device, mesh=mesh, in_specs=in_specs, out_specs=out_specs, check_vma=False
    )
```

```python
import functools

import jax
import jax.numpy as jnp
from jax import lax
from jax.experimental import pallas as pl
from jax.experimental.pallas import tpu as pltpu
from jax.sharding import PartitionSpec as P

MESH = pl.DeviceIdType.MESH
F32 = jnp.float32
BF16 = jnp.bfloat16


def dot_nt(left, right):
    return lax.dot_general(left, right, (((1,), (1,)), ((), ())), preferred_element_type=F32)


def kernel(
    nbub,
    npan,
    groups,
    dens_ref,
    rhs_ref,
    inv_hbm,
    near_hbm,
    src_bubble_ref,
    src_block_ref,
    count_ref,
    colour_ref,
    mom_hbm,
    spread_hbm,
    centres_ref,
    out_ref,
    near_v,
    inv_v,
    mom_v,
    spread_v,
    hood,
    onehot,
    picked,
    part_mom,
    all_mom,
    green,
    far_v,
    near_sem,
    inv_sem,
    map_sem,
    dens_send,
    dens_recv,
    part_send,
    part_recv,
    mom_send,
    mom_recv,
):
    bub, panels = dens_ref.shape
    rows, slots, blk = near_v.shape[1], near_v.shape[2], near_v.shape[3]
    pairs = rows // 2
    chunk = rows * bub
    moments = mom_v.shape[0] // bub
    lanes = bub * moments
    peers = 3 * npan
    group_pairs = pairs // groups
    me_b, me_p = lax.axis_index("bubble"), lax.axis_index("panel")
    own_slot = npan + me_p

    def rows_of(slot, first, size):
        return pl.ds(pl.multiple_of(slot * chunk + first, 16), size)

    def cols(first, size):
        return pl.ds(pl.multiple_of(first, 128), size)

    def for_peers(do):
        def step(j, carry):
            side, p = j // npan, lax.rem(j, npan)
            other = me_b + side - 1
            ok = (other >= 0) & (other < nbub) & jnp.logical_not((side == 1) & (p == me_p))

            @pl.when(ok)
            def _():
                do(j, side, p, other)

            return carry

        lax.fori_loop(0, peers, step, 0)

    def for_others(count, me, do):
        def step(j, carry):
            @pl.when(j != me)
            def _():
                do(j)

            return carry

        lax.fori_loop(0, count, step, 0)

    barrier = pltpu.get_barrier_semaphore()

    def greet(j, side, p, other):
        pl.semaphore_signal(barrier, inc=1, device_id=(other, p), device_id_type=MESH)

    def greet_bubble(j):
        pl.semaphore_signal(barrier, inc=1, device_id=(j, me_p), device_id_type=MESH)

    for_peers(greet)
    for_others(nbub, me_b, greet_bubble)

    mom_copy = pltpu.make_async_copy(mom_hbm, mom_v, map_sem.at[0])
    spread_copy = pltpu.make_async_copy(spread_hbm, spread_v, map_sem.at[1])
    mom_copy.start()

    def near_copy(q):
        two = pl.ds(2 * q, 2)
        return pltpu.make_async_copy(near_hbm.at[:, two], near_v.at[:, two], near_sem.at[q])

    def inv_copy(q):
        two = pl.ds(2 * q, 2)
        return pltpu.make_async_copy(inv_hbm.at[:, two], inv_v.at[:, two], inv_sem.at[q])

    def start_load(q, carry):
        near_copy(q).start()
        inv_copy(q).start()
        return carry

    lax.fori_loop(0, 1, start_load, 0)
    spread_copy.start()
    lax.fori_loop(1, pairs, start_load, 0)

    def place(q, carry):
        both = jnp.concatenate(
            [dens_ref[:, cols(2 * q * blk, blk)], dens_ref[:, cols((2 * q + 1) * blk, blk)]], axis=0
        )
        hood[0, rows_of(own_slot, q * 16, 16), :] = both.astype(BF16)
        return carry

    lax.fori_loop(0, pairs, place, 0)

    @pl.when(me_b == 0)
    def _():
        hood[:, pl.ds(0, npan * chunk), :] = jnp.zeros((2, npan * chunk, blk), BF16)

    @pl.when(me_b == nbub - 1)
    def _():
        hood[:, pl.ds(2 * npan * chunk, npan * chunk), :] = jnp.zeros((2, npan * chunk, blk), BF16)

    sides = (me_b > 0).astype(jnp.int32) + (me_b < nbub - 1).astype(jnp.int32)
    pl.semaphore_wait(barrier, npan - 1 + npan * sides + nbub - 1)

    def dens_copy(sem, phase, first, size, j, side, p, other):
        piece = hood.at[phase, rows_of(own_slot, first, size)]
        back = (2 - side) * npan + me_p
        return pltpu.make_async_remote_copy(
            src_ref=piece,
            dst_ref=hood.at[phase, rows_of(back, first, size)],
            send_sem=dens_send.at[sem, j],
            recv_sem=dens_recv.at[sem, back],
            device_id=(other, p),
            device_id_type=MESH,
        )

    def dens_arrival(sem, phase, first, size, j, side, p, other):
        piece = hood.at[phase, rows_of(j, first, size)]
        return pltpu.make_async_remote_copy(
            src_ref=piece,
            dst_ref=piece,
            send_sem=dens_send.at[sem, j],
            recv_sem=dens_recv.at[sem, j],
            device_id=(other, p),
            device_id_type=MESH,
        )

    def part_copy(phase, slot, p):
        return pltpu.make_async_remote_copy(
            src_ref=part_mom.at[phase, me_p],
            dst_ref=part_mom.at[phase, slot],
            send_sem=part_send.at[phase, p],
            recv_sem=part_recv.at[phase, slot],
            device_id=(me_b, p),
            device_id_type=MESH,
        )

    def mom_copy_to(phase, slot, b):
        return pltpu.make_async_remote_copy(
            src_ref=all_mom.at[phase, me_b],
            dst_ref=all_mom.at[phase, slot],
            send_sem=mom_send.at[phase, b],
            recv_sem=mom_recv.at[phase, slot],
            device_id=(b, me_p),
            device_id_type=MESH,
        )

    group_rows = group_pairs * 16
    pieces = [(0, 0, 0, chunk)] + [(1 + g, 1, g * group_rows, group_rows) for g in range(groups)]

    for_peers(lambda *a: dens_copy(*pieces[0], *a).start())

    lane = lax.broadcasted_iota(jnp.int32, (bub, lanes), 1)
    row = lax.broadcasted_iota(jnp.int32, (bub, lanes), 0)
    diagonal = lane // moments == row

    def send_moments(phase, source):
        partial = jnp.where(diagonal, dot_nt(source[...].astype(BF16), mom_v[...]), 0.0)
        total = jnp.sum(partial, axis=0, keepdims=True)
        part_mom[phase, me_p] = jnp.broadcast_to(total, (bub, lanes))
        for_others(npan, me_p, lambda p: part_copy(phase, me_p, p).start())

    def pass_moments(phase):
        for_others(npan, me_p, lambda p: part_copy(phase, p, p).wait_recv())
        total = part_mom[phase, 0]
        for p in range(1, npan):
            total = total + part_mom[phase, p]
        all_mom[phase, me_b] = total
        for_others(nbub, me_b, lambda b: mom_copy_to(phase, me_b, b).start())

    def far_field(phase):
        for_others(nbub, me_b, lambda b: mom_copy_to(phase, b, b).wait_recv())
        total = green[0] * all_mom[phase, 0]
        for b in range(1, nbub):
            total = total + green[b] * all_mom[phase, b]
        shift = moments
        while shift < lanes:
            total = total + pltpu.roll(total, shift, 1)
            shift *= 2
        coeff = jnp.where(diagonal, total, 0.0).astype(BF16)
        far_v[...] = jnp.dot(coeff, spread_v[...], preferred_element_type=F32)

    mom_copy.wait()
    send_moments(0, dens_ref)

    def build(b, carry):
        on = lax.broadcasted_iota(jnp.int32, (rows, rows), 0) == lax.broadcasted_iota(
            jnp.int32, (rows, rows), 1
        )
        near_bub = src_bubble_ref[b] - (me_b * bub - bub)
        block = src_block_ref[b]
        index = (near_bub // bub * npan + block // rows) * chunk
        index = index + lax.rem(block, rows) * bub + lax.rem(near_bub, bub)
        slot = lax.broadcasted_iota(jnp.int32, (slots, rows), 0)
        index = jnp.where(slot < count_ref[pl.ds(b, 1), :], index, -1).astype(F32)
        wide = jnp.concatenate(
            [
                jnp.sum(
                    jnp.where(on, jnp.broadcast_to(index[s : s + 1, :], (rows, rows)), 0.0),
                    axis=1,
                    keepdims=True,
                )
                for s in range(slots)
            ],
            axis=0,
        )
        wide = jnp.broadcast_to(wide, (slots * rows, 128))
        place_of = lax.broadcasted_iota(jnp.int32, (slots * rows, 128), 1).astype(F32)
        mine_rows = pl.ds(pl.multiple_of(b * slots * rows, 16), slots * rows)
        for c in range(peers * chunk // 128):
            hit = wide == place_of + float(c * 128)
            onehot[mine_rows, c * 128 : (c + 1) * 128] = jnp.where(hit, 1.0, 0.0).astype(BF16)
        return carry

    lax.fori_loop(0, bub, build, 0)

    which = lax.broadcasted_iota(jnp.int32, (bub, nbub * bub), 1)
    mine = which == me_b * bub + lax.broadcasted_iota(jnp.int32, (bub, nbub * bub), 0)
    own = [
        jnp.sum(jnp.where(mine, centres_ref[c : c + 1, :], 0.0), axis=1, keepdims=True)
        for c in range(3)
    ]
    spot = lax.broadcasted_iota(jnp.int32, (nbub * bub, lanes), 0)
    over = lax.broadcasted_iota(jnp.int32, (nbub * bub, lanes), 1) // moments
    for b in range(nbub):
        spread_out = jnp.where(spot == over + b * bub, 1.0, 0.0)
        wide = jnp.dot(
            centres_ref[...], spread_out, precision=lax.Precision.HIGHEST, preferred_element_type=F32
        )
        dx, dy, dz = [own[c] - wide[c : c + 1, :] for c in range(3)]
        flat = dx * dx + dy * dy
        up = own[2] + wide[2:3, :]
        value = 1.0 / jnp.sqrt(flat + dz * dz + 1.0) + 1.0 / jnp.sqrt(flat + up * up + 1.0)
        gap = jnp.abs(me_b * bub + row - (b * bub + lane // moments))
        green[b] = jnp.where(gap > bub, value, 0.0)

    tint = jnp.zeros((bub, blk), jnp.int32)
    line = lax.broadcasted_iota(jnp.int32, (bub, blk), 0)
    for b in range(bub):
        tint = jnp.where(line == b, colour_ref[b], tint)

    pass_moments(0)

    def pick(phase):
        size = slots * rows
        half = bub // 2

        def step(h, carry):
            some = onehot[pl.ds(pl.multiple_of(h * half * size, 16), half * size), :]
            got = jnp.dot(some, hood[phase], preferred_element_type=F32)
            for o in range(half):
                picked[pl.ds(h * half + o, size, stride=bub), :] = got[o * size : (o + 1) * size]
            return carry

        lax.fori_loop(0, 2, step, 0)

    line_two = lax.rem(lax.broadcasted_iota(jnp.int32, (2 * bub, blk), 0), bub)

    def by_bubble(parts, right_of, count):
        total = None
        for first in range(0, bub, count):
            some = range(first, first + count)
            left = jnp.concatenate(
                [jnp.where(line_two == b, part, 0.0) for b in some for part in parts], axis=1
            )
            right = jnp.concatenate([right_of(b) for b in some], axis=1)
            got = dot_nt(left.astype(BF16), right)
            total = got if total is None else total + got
        return jnp.concatenate([total[:bub, :blk], total[bub:, blk:]], axis=0)

    def stacked(ref, q):
        first, second = cols(2 * q * blk, blk), cols((2 * q + 1) * blk, blk)
        return jnp.concatenate([ref[:, first], ref[:, second]], axis=0)

    def near_block(b, q):
        return jnp.concatenate(
            [
                jnp.concatenate([near_v[b, 2 * q + o, s] for s in range(slots)], axis=1)
                for o in range(2)
            ],
            axis=0,
        )

    def inv_block(b, q):
        return jnp.concatenate([inv_v[b, 2 * q], inv_v[b, 2 * q + 1]], axis=0)

    both_tint = jnp.concatenate([tint, tint], axis=0)

    def solve(phase, old_ref, some):
        rests = []
        for q in some:
            parts = [
                picked[pl.ds(pl.multiple_of((s * rows + 2 * q) * bub, 16), 16), :]
                for s in range(slots)
            ]
            near = by_bubble(parts, lambda b: near_block(b, q), 2)
            rests.append(stacked(rhs_ref, q) - near - stacked(far_v, q))
        news = []
        for q, rest in zip(some, rests):
            updated = by_bubble([rest], lambda b: inv_block(b, q), bub)
            news.append(jnp.where(both_tint == phase, updated, stacked(old_ref, q)))
        for q, new in zip(some, news):
            out_ref[:, cols(2 * q * blk, blk)] = new[:bub]
            out_ref[:, cols((2 * q + 1) * blk, blk)] = new[bub:]
        return news

    spread_copy.wait()
    for_peers(lambda *a: dens_arrival(*pieces[0], *a).wait_recv())
    pick(0)
    far_field(0)
    batch = 2 if group_pairs % 2 == 0 else 1

    def first_colour(t, carry):
        some = [batch * t + o for o in range(batch)]
        for q in some:
            near_copy(q).wait()
            inv_copy(q).wait()
        for q, new in zip(some, solve(0, dens_ref, some)):
            hood[1, rows_of(own_slot, q * 16, 16), :] = new.astype(BF16)
        return carry

    steps = group_pairs // batch
    for g in range(groups):
        lax.fori_loop(g * steps, (g + 1) * steps, first_colour, 0)
        for_peers(lambda *a: dens_copy(*pieces[1 + g], *a).start())

    send_moments(1, out_ref)
    pass_moments(1)
    for g in range(groups):
        for_peers(lambda *a: dens_arrival(*pieces[1 + g], *a).wait_recv())
    pick(1)
    far_field(1)

    def second_colour(t, carry):
        solve(1, out_ref, [batch * t + o for o in range(batch)])
        return carry

    lax.fori_loop(0, pairs // batch, second_colour, 0)

    for piece in pieces:
        for_peers(lambda *a: dens_copy(*piece, *a).wait_send())
    for phase in range(2):
        for_others(npan, me_p, lambda p: part_copy(phase, me_p, p).wait_send())
        for_others(nbub, me_b, lambda b: mom_copy_to(phase, me_b, b).wait_send())


def per_device(
    density,
    right_side,
    inv_diag,
    near_vals,
    near_bubble,
    near_block,
    near_count,
    colour,
    moment_map,
    spread_map,
    centres,
):
    nbub, npan = lax.axis_size("bubble"), lax.axis_size("panel")
    bub, panels = density.shape
    rows, slots, blk = near_vals.shape[1:4]
    moments = moment_map.shape[1]
    lanes = bub * moments
    groups = 3 if (rows // 2) % 3 == 0 else 1
    pairs = rows // 2
    chunk = rows * bub
    hood_rows = 3 * npan * chunk
    vmem = pl.BlockSpec(memory_space=pltpu.VMEM)
    smem = pl.BlockSpec(memory_space=pltpu.SMEM)
    hbm = pl.BlockSpec(memory_space=pl.ANY)
    dma = pltpu.SemaphoreType.DMA
    return pl.pallas_call(
        functools.partial(kernel, nbub, npan, groups),
        out_shape=jax.ShapeDtypeStruct(density.shape, F32),
        in_specs=[vmem, vmem, hbm, hbm, vmem, vmem, vmem, smem, hbm, hbm, vmem],
        out_specs=vmem,
        scratch_shapes=[
            pltpu.VMEM(near_vals.shape, BF16),
            pltpu.VMEM(inv_diag.shape, BF16),
            pltpu.VMEM((lanes, panels), BF16),
            pltpu.VMEM((lanes, panels), BF16),
            pltpu.VMEM((2, hood_rows, blk), BF16),
            pltpu.VMEM((bub * slots * rows, hood_rows), BF16),
            pltpu.VMEM((slots * rows * bub, blk), F32),
            pltpu.VMEM((2, npan, bub, lanes), F32),
            pltpu.VMEM((2, nbub, bub, lanes), F32),
            pltpu.VMEM((nbub, bub, lanes), F32),
            pltpu.VMEM((bub, panels), F32),
            dma((pairs,)),
            dma((pairs,)),
            dma((2,)),
            dma((1 + groups, 3 * npan)),
            dma((1 + groups, 3 * npan)),
            dma((2, npan)),
            dma((2, npan)),
            dma((2, nbub)),
            dma((2, nbub)),
        ],
        compiler_params=pltpu.CompilerParams(
            collective_id=0, has_side_effects=True, vmem_limit_bytes=56 * 1024 * 1024
        ),
    )(
        density,
        right_side,
        inv_diag,
        near_vals,
        near_bubble.transpose(0, 2, 1),
        near_block.transpose(0, 2, 1),
        near_count,
        colour,
        moment_map.reshape(lanes, panels),
        spread_map.reshape(lanes, panels),
        centres,
    )


def solution(mesh):
    in_specs = (
        P("bubble", "panel"),
        P("bubble", "panel"),
        P("bubble", "panel", None, None),
        P("bubble", "panel", None, None, None),
        P("bubble", "panel", None),
        P("bubble", "panel", None),
        P("bubble", "panel"),
        P("bubble"),
        P("bubble", None, "panel"),
        P("bubble", None, "panel"),
        P(),
    )
    out_specs = P("bubble", "panel")
    return jax.shard_map(
        per_device, mesh=mesh, in_specs=in_specs, out_specs=out_specs, check_vma=False
    )
```

```python
import functools

import jax
import jax.numpy as jnp
from jax import lax
from jax.experimental import pallas as pl
from jax.experimental.pallas import tpu as pltpu
from jax.sharding import PartitionSpec as P

MESH = pl.DeviceIdType.MESH
F32 = jnp.float32
BF16 = jnp.bfloat16


def dot_nt(left, right):
    return lax.dot_general(left, right, (((1,), (1,)), ((), ())), preferred_element_type=F32)


def kernel(
    nbub,
    npan,
    groups,
    dens_ref,
    rhs_ref,
    inv_hbm,
    near_hbm,
    src_bubble_ref,
    src_block_ref,
    count_ref,
    colour_ref,
    mom_hbm,
    spread_hbm,
    centres_ref,
    out_ref,
    near_v,
    inv_v,
    mom_v,
    spread_v,
    hood,
    onehot,
    picked,
    part_mom,
    all_mom,
    green,
    far_v,
    near_sem,
    inv_sem,
    map_sem,
    halo_send,
    cross_send,
    core_send,
    direct_send,
    dens_recv,
    part_send,
    part_recv,
    mom_send,
    mom_recv,
):
    bub, panels = dens_ref.shape
    rows, slots, blk = near_v.shape[1], near_v.shape[2], near_v.shape[3]
    pairs = rows // 2
    chunk = rows * bub
    moments = mom_v.shape[0] // bub
    lanes = bub * moments
    peers = 3 * npan
    group_pairs = pairs // groups
    me_b, me_p = lax.axis_index("bubble"), lax.axis_index("panel")
    own_slot = npan + me_p

    def rows_of(slot, first, size):
        return pl.ds(pl.multiple_of(slot * chunk + first, 16), size)

    def cols(first, size):
        return pl.ds(pl.multiple_of(first, 128), size)

    def for_peers(do):
        def step(j, carry):
            side, p = j // npan, lax.rem(j, npan)
            other = me_b + side - 1
            ok = (other >= 0) & (other < nbub) & jnp.logical_not((side == 1) & (p == me_p))

            @pl.when(ok)
            def _():
                do(j, side, p, other)

            return carry

        lax.fori_loop(0, peers, step, 0)

    def for_others(count, me, do):
        def step(j, carry):
            @pl.when(j != me)
            def _():
                do(j)

            return carry

        lax.fori_loop(0, count, step, 0)

    barrier = pltpu.get_barrier_semaphore()

    def greet(j, side, p, other):
        pl.semaphore_signal(barrier, inc=1, device_id=(other, p), device_id_type=MESH)

    def greet_bubble(j):
        pl.semaphore_signal(barrier, inc=1, device_id=(j, me_p), device_id_type=MESH)

    for_peers(greet)
    for_others(nbub, me_b, greet_bubble)

    mom_copy = pltpu.make_async_copy(mom_hbm, mom_v, map_sem.at[0])
    spread_copy = pltpu.make_async_copy(spread_hbm, spread_v, map_sem.at[1])
    mom_copy.start()

    def near_copy(q):
        two = pl.ds(2 * q, 2)
        return pltpu.make_async_copy(near_hbm.at[:, two], near_v.at[:, two], near_sem.at[q])

    def inv_copy(q):
        two = pl.ds(2 * q, 2)
        return pltpu.make_async_copy(inv_hbm.at[:, two], inv_v.at[:, two], inv_sem.at[q])

    def start_load(q, carry):
        near_copy(q).start()
        inv_copy(q).start()
        return carry

    lax.fori_loop(0, 1, start_load, 0)
    spread_copy.start()
    lax.fori_loop(1, pairs, start_load, 0)

    def place(q, carry):
        both = jnp.concatenate(
            [dens_ref[:, cols(2 * q * blk, blk)], dens_ref[:, cols((2 * q + 1) * blk, blk)]], axis=0
        )
        hood[0, rows_of(own_slot, q * 16, 16), :] = both.astype(BF16)
        return carry

    lax.fori_loop(0, pairs, place, 0)

    @pl.when(me_b == 0)
    def _():
        hood[:, pl.ds(0, npan * chunk), :] = jnp.zeros((2, npan * chunk, blk), BF16)

    @pl.when(me_b == nbub - 1)
    def _():
        hood[:, pl.ds(2 * npan * chunk, npan * chunk), :] = jnp.zeros((2, npan * chunk, blk), BF16)

    sides = (me_b > 0).astype(jnp.int32) + (me_b < nbub - 1).astype(jnp.int32)
    pl.semaphore_wait(barrier, npan - 1 + npan * sides + nbub - 1)

    group_rows = group_pairs * 16
    pieces = [(0, 0, chunk)] + [(1, g * group_rows, group_rows) for g in range(groups)]
    last = groups
    parity = lax.rem(me_p, 2)
    partner = me_p + 1 - 2 * parity

    def dens_copy(e, source, target, send, other, p):
        phase, first, size = pieces[e]
        return pltpu.make_async_remote_copy(
            src_ref=hood.at[phase, rows_of(source, first, size)],
            dst_ref=hood.at[phase, rows_of(target, first, size)],
            send_sem=send,
            recv_sem=dens_recv.at[e, target],
            device_id=(other, p),
            device_id_type=MESH,
        )

    def arrive(e, slot):
        dens_copy(e, slot, slot, direct_send.at[0], me_b, partner).wait_recv()

    def where_side(side, do):
        if side == 1:
            do()
        else:
            pl.when(me_b > 0 if side == 0 else me_b < nbub - 1)(do)

    def halo(e, act):
        for side in (0, 2):
            target = (2 - side) * npan + me_p
            where_side(
                side,
                lambda: act(
                    dens_copy(
                        e, own_slot, target, halo_send.at[e, side], me_b + side - 1, me_p
                    )
                ),
            )

    def cross(e, side, act):
        slot = side * npan + me_p
        for i in range(npan // 2):
            p = 2 * i + parity

            @pl.when(p != me_p)
            def _():
                act(dens_copy(e, slot, slot, cross_send.at[e, side, i], me_b, p))

    def core(e, slot, act):
        act(dens_copy(e, slot, slot, core_send.at[e, slot], me_b, partner))

    def first_hop(e):
        halo(e, lambda c: c.start())
        cross(e, 1, lambda c: c.start())
        core(e, own_slot, lambda c: c.start())

    def second_hop(e):
        for side in (0, 2):

            def pass_on():
                slot = side * npan + me_p
                arrive(e, slot)
                cross(e, side, lambda c: c.start())
                core(e, slot, lambda c: c.start())

            where_side(side, pass_on)

    def third_hop(e):
        for side in (1, 0, 2):
            for i in range(npan // 2):
                p = 2 * i + parity

                def pass_on():
                    slot = side * npan + p
                    arrive(e, slot)
                    core(e, slot, lambda c: c.start())

                where_side(side, lambda: pl.when(p != me_p)(pass_on))

    def last_arrivals(e):
        for side in (1, 0, 2):
            for i in range(npan // 2):
                slot = side * npan + 2 * i + 1 - parity
                where_side(side, lambda: arrive(e, slot))

    def sends_done(e):
        halo(e, lambda c: c.wait_send())
        for side in range(3):

            def done():
                cross(e, side, lambda c: c.wait_send())
                for i in range(npan // 2):
                    core(e, side * npan + 2 * i + parity, lambda c: c.wait_send())

            where_side(side, done)

    def direct(act):
        def one(j, side, p, other):
            target = (2 - side) * npan + me_p
            act(dens_copy(last, own_slot, target, direct_send.at[j], other, p))

        for_peers(one)

    def part_copy(phase, slot, p):
        return pltpu.make_async_remote_copy(
            src_ref=part_mom.at[phase, me_p],
            dst_ref=part_mom.at[phase, slot],
            send_sem=part_send.at[phase, p],
            recv_sem=part_recv.at[phase, slot],
            device_id=(me_b, p),
            device_id_type=MESH,
        )

    def mom_copy_to(phase, slot, b):
        return pltpu.make_async_remote_copy(
            src_ref=all_mom.at[phase, me_b],
            dst_ref=all_mom.at[phase, slot],
            send_sem=mom_send.at[phase, b],
            recv_sem=mom_recv.at[phase, slot],
            device_id=(b, me_p),
            device_id_type=MESH,
        )

    first_hop(0)

    lane = lax.broadcasted_iota(jnp.int32, (bub, lanes), 1)
    row = lax.broadcasted_iota(jnp.int32, (bub, lanes), 0)
    diagonal = lane // moments == row

    def send_moments(phase, source):
        partial = jnp.where(diagonal, dot_nt(source[...].astype(BF16), mom_v[...]), 0.0)
        total = jnp.sum(partial, axis=0, keepdims=True)
        part_mom[phase, me_p] = jnp.broadcast_to(total, (bub, lanes))
        for_others(npan, me_p, lambda p: part_copy(phase, me_p, p).start())

    def pass_moments(phase):
        for_others(npan, me_p, lambda p: part_copy(phase, p, p).wait_recv())
        total = part_mom[phase, 0]
        for p in range(1, npan):
            total = total + part_mom[phase, p]
        all_mom[phase, me_b] = total
        for_others(nbub, me_b, lambda b: mom_copy_to(phase, me_b, b).start())

    def far_field(phase):
        for_others(nbub, me_b, lambda b: mom_copy_to(phase, b, b).wait_recv())
        total = green[0] * all_mom[phase, 0]
        for b in range(1, nbub):
            total = total + green[b] * all_mom[phase, b]
        shift = moments
        while shift < lanes:
            total = total + pltpu.roll(total, shift, 1)
            shift *= 2
        coeff = jnp.where(diagonal, total, 0.0).astype(BF16)
        far_v[...] = jnp.dot(coeff, spread_v[...], preferred_element_type=F32)

    mom_copy.wait()
    send_moments(0, dens_ref)

    def build(b, carry):
        on = lax.broadcasted_iota(jnp.int32, (rows, rows), 0) == lax.broadcasted_iota(
            jnp.int32, (rows, rows), 1
        )
        near_bub = src_bubble_ref[b] - (me_b * bub - bub)
        block = src_block_ref[b]
        index = (near_bub // bub * npan + block // rows) * chunk
        index = index + lax.rem(block, rows) * bub + lax.rem(near_bub, bub)
        slot = lax.broadcasted_iota(jnp.int32, (slots, rows), 0)
        index = jnp.where(slot < count_ref[pl.ds(b, 1), :], index, -1).astype(F32)
        wide = jnp.concatenate(
            [
                jnp.sum(
                    jnp.where(on, jnp.broadcast_to(index[s : s + 1, :], (rows, rows)), 0.0),
                    axis=1,
                    keepdims=True,
                )
                for s in range(slots)
            ],
            axis=0,
        )
        wide = jnp.broadcast_to(wide, (slots * rows, 128))
        place_of = lax.broadcasted_iota(jnp.int32, (slots * rows, 128), 1).astype(F32)
        mine_rows = pl.ds(pl.multiple_of(b * slots * rows, 16), slots * rows)
        for c in range(peers * chunk // 128):
            hit = wide == place_of + float(c * 128)
            onehot[mine_rows, c * 128 : (c + 1) * 128] = jnp.where(hit, 1.0, 0.0).astype(BF16)
        return carry

    lax.fori_loop(0, bub // 2, build, 0)
    second_hop(0)
    lax.fori_loop(bub // 2, bub, build, 0)
    third_hop(0)

    which = lax.broadcasted_iota(jnp.int32, (bub, nbub * bub), 1)
    mine = which == me_b * bub + lax.broadcasted_iota(jnp.int32, (bub, nbub * bub), 0)
    own = [
        jnp.sum(jnp.where(mine, centres_ref[c : c + 1, :], 0.0), axis=1, keepdims=True)
        for c in range(3)
    ]
    spot = lax.broadcasted_iota(jnp.int32, (nbub * bub, lanes), 0)
    over = lax.broadcasted_iota(jnp.int32, (nbub * bub, lanes), 1) // moments
    for b in range(nbub):
        spread_out = jnp.where(spot == over + b * bub, 1.0, 0.0)
        wide = jnp.dot(
            centres_ref[...], spread_out, precision=lax.Precision.HIGHEST, preferred_element_type=F32
        )
        dx, dy, dz = [own[c] - wide[c : c + 1, :] for c in range(3)]
        flat = dx * dx + dy * dy
        up = own[2] + wide[2:3, :]
        value = 1.0 / jnp.sqrt(flat + dz * dz + 1.0) + 1.0 / jnp.sqrt(flat + up * up + 1.0)
        gap = jnp.abs(me_b * bub + row - (b * bub + lane // moments))
        green[b] = jnp.where(gap > bub, value, 0.0)

    tint = jnp.zeros((bub, blk), jnp.int32)
    line = lax.broadcasted_iota(jnp.int32, (bub, blk), 0)
    for b in range(bub):
        tint = jnp.where(line == b, colour_ref[b], tint)

    pass_moments(0)

    def pick(phase):
        size = slots * rows
        half = bub // 2

        def step(h, carry):
            some = onehot[pl.ds(pl.multiple_of(h * half * size, 16), half * size), :]
            got = jnp.dot(some, hood[phase], preferred_element_type=F32)
            for o in range(half):
                picked[pl.ds(h * half + o, size, stride=bub), :] = got[o * size : (o + 1) * size]
            return carry

        lax.fori_loop(0, 2, step, 0)

    line_two = lax.rem(lax.broadcasted_iota(jnp.int32, (2 * bub, blk), 0), bub)

    def by_bubble(parts, right_of, count):
        total = None
        for first in range(0, bub, count):
            some = range(first, first + count)
            left = jnp.concatenate(
                [jnp.where(line_two == b, part, 0.0) for b in some for part in parts], axis=1
            )
            right = jnp.concatenate([right_of(b) for b in some], axis=1)
            got = dot_nt(left.astype(BF16), right)
            total = got if total is None else total + got
        return jnp.concatenate([total[:bub, :blk], total[bub:, blk:]], axis=0)

    def stacked(ref, q):
        first, second = cols(2 * q * blk, blk), cols((2 * q + 1) * blk, blk)
        return jnp.concatenate([ref[:, first], ref[:, second]], axis=0)

    def near_block(b, q):
        return jnp.concatenate(
            [
                jnp.concatenate([near_v[b, 2 * q + o, s] for s in range(slots)], axis=1)
                for o in range(2)
            ],
            axis=0,
        )

    def inv_block(b, q):
        return jnp.concatenate([inv_v[b, 2 * q], inv_v[b, 2 * q + 1]], axis=0)

    both_tint = jnp.concatenate([tint, tint], axis=0)

    def solve(phase, old_ref, some):
        rests = []
        for q in some:
            parts = [
                picked[pl.ds(pl.multiple_of((s * rows + 2 * q) * bub, 16), 16), :]
                for s in range(slots)
            ]
            near = by_bubble(parts, lambda b: near_block(b, q), 2)
            rests.append(stacked(rhs_ref, q) - near - stacked(far_v, q))
        news = []
        for q, rest in zip(some, rests):
            updated = by_bubble([rest], lambda b: inv_block(b, q), bub)
            news.append(jnp.where(both_tint == phase, updated, stacked(old_ref, q)))
        for q, new in zip(some, news):
            out_ref[:, cols(2 * q * blk, blk)] = new[:bub]
            out_ref[:, cols((2 * q + 1) * blk, blk)] = new[bub:]
        return news

    spread_copy.wait()
    last_arrivals(0)
    pick(0)
    far_field(0)
    batch = 2 if group_pairs % 2 == 0 else 1

    def first_colour(t, carry):
        some = [batch * t + o for o in range(batch)]
        for q in some:
            near_copy(q).wait()
            inv_copy(q).wait()
        for q, new in zip(some, solve(0, dens_ref, some)):
            hood[1, rows_of(own_slot, q * 16, 16), :] = new.astype(BF16)
        return carry

    steps = group_pairs // batch
    total_steps = groups * steps

    def first_steps(t, carry):
        first_colour(t, carry)
        for g in range(groups - 1):
            for hop, do in enumerate((first_hop, second_hop, third_hop)):
                if (g + 1) * steps - 1 + hop < total_steps:
                    pl.when(t == (g + 1) * steps - 1 + hop)(functools.partial(do, 1 + g))
        return carry

    lax.fori_loop(0, total_steps, first_steps, 0)
    direct(lambda c: c.start())
    send_moments(1, out_ref)
    pass_moments(1)
    for g in range(groups - 1):
        for hop, do in enumerate((first_hop, second_hop, third_hop)):
            if (g + 1) * steps - 1 + hop >= total_steps:
                do(1 + g)
    for g in range(groups - 1):
        last_arrivals(1 + g)
    for_peers(lambda j, side, p, other: arrive(last, j))
    pick(1)
    far_field(1)

    def second_colour(t, carry):
        solve(1, out_ref, [batch * t + o for o in range(batch)])
        return carry

    lax.fori_loop(0, pairs // batch, second_colour, 0)

    for e in range(groups):
        sends_done(e)
    direct(lambda c: c.wait_send())
    for phase in range(2):
        for_others(npan, me_p, lambda p: part_copy(phase, me_p, p).wait_send())
        for_others(nbub, me_b, lambda b: mom_copy_to(phase, me_b, b).wait_send())


def per_device(
    density,
    right_side,
    inv_diag,
    near_vals,
    near_bubble,
    near_block,
    near_count,
    colour,
    moment_map,
    spread_map,
    centres,
):
    nbub, npan = lax.axis_size("bubble"), lax.axis_size("panel")
    bub, panels = density.shape
    rows, slots, blk = near_vals.shape[1:4]
    moments = moment_map.shape[1]
    lanes = bub * moments
    groups = 3 if (rows // 2) % 3 == 0 else 1
    pairs = rows // 2
    chunk = rows * bub
    hood_rows = 3 * npan * chunk
    vmem = pl.BlockSpec(memory_space=pltpu.VMEM)
    smem = pl.BlockSpec(memory_space=pltpu.SMEM)
    hbm = pl.BlockSpec(memory_space=pl.ANY)
    dma = pltpu.SemaphoreType.DMA
    return pl.pallas_call(
        functools.partial(kernel, nbub, npan, groups),
        out_shape=jax.ShapeDtypeStruct(density.shape, F32),
        in_specs=[vmem, vmem, hbm, hbm, vmem, vmem, vmem, smem, hbm, hbm, vmem],
        out_specs=vmem,
        scratch_shapes=[
            pltpu.VMEM(near_vals.shape, BF16),
            pltpu.VMEM(inv_diag.shape, BF16),
            pltpu.VMEM((lanes, panels), BF16),
            pltpu.VMEM((lanes, panels), BF16),
            pltpu.VMEM((2, hood_rows, blk), BF16),
            pltpu.VMEM((bub * slots * rows, hood_rows), BF16),
            pltpu.VMEM((slots * rows * bub, blk), F32),
            pltpu.VMEM((2, npan, bub, lanes), F32),
            pltpu.VMEM((2, nbub, bub, lanes), F32),
            pltpu.VMEM((nbub, bub, lanes), F32),
            pltpu.VMEM((bub, panels), F32),
            dma((pairs,)),
            dma((pairs,)),
            dma((2,)),
            dma((1 + groups, 3)),
            dma((1 + groups, 3, npan // 2)),
            dma((1 + groups, 3 * npan)),
            dma((3 * npan,)),
            dma((1 + groups, 3 * npan)),
            dma((2, npan)),
            dma((2, npan)),
            dma((2, nbub)),
            dma((2, nbub)),
        ],
        compiler_params=pltpu.CompilerParams(
            collective_id=0, has_side_effects=True, vmem_limit_bytes=56 * 1024 * 1024
        ),
    )(
        density,
        right_side,
        inv_diag,
        near_vals,
        near_bubble.transpose(0, 2, 1),
        near_block.transpose(0, 2, 1),
        near_count,
        colour,
        moment_map.reshape(lanes, panels),
        spread_map.reshape(lanes, panels),
        centres,
    )


def solution(mesh):
    in_specs = (
        P("bubble", "panel"),
        P("bubble", "panel"),
        P("bubble", "panel", None, None),
        P("bubble", "panel", None, None, None),
        P("bubble", "panel", None),
        P("bubble", "panel", None),
        P("bubble", "panel"),
        P("bubble"),
        P("bubble", None, "panel"),
        P("bubble", None, "panel"),
        P(),
    )
    out_specs = P("bubble", "panel")
    return jax.shard_map(
        per_device, mesh=mesh, in_specs=in_specs, out_specs=out_specs, check_vma=False
    )
```

```python
import functools

import jax
import jax.numpy as jnp
from jax import lax
from jax.experimental import pallas as pl
from jax.experimental.pallas import tpu as pltpu
from jax.sharding import PartitionSpec as P

MESH = pl.DeviceIdType.MESH
F32 = jnp.float32
BF16 = jnp.bfloat16


def dot_nt(left, right):
    return lax.dot_general(left, right, (((1,), (1,)), ((), ())), preferred_element_type=F32)


def kernel(
    nbub,
    npan,
    groups,
    dens_ref,
    rhs_ref,
    inv_hbm,
    near_hbm,
    src_bubble_ref,
    src_block_ref,
    count_ref,
    colour_ref,
    mom_hbm,
    spread_hbm,
    centres_ref,
    out_ref,
    near_v,
    inv_v,
    mom_v,
    spread_v,
    hood,
    onehot,
    picked,
    part_mom,
    all_mom,
    green,
    far_v,
    near_sem,
    inv_sem,
    map_sem,
    dens_send,
    dens_recv,
    part_send,
    part_recv,
    mom_send,
    mom_recv,
):
    bub, panels = dens_ref.shape
    rows, slots, blk = near_v.shape[1], near_v.shape[2], near_v.shape[3]
    pairs = rows // 2
    chunk = rows * bub
    moments = mom_v.shape[0] // bub
    lanes = bub * moments
    peers = 3 * npan
    group_pairs = pairs // groups
    me_b, me_p = lax.axis_index("bubble"), lax.axis_index("panel")
    own_slot = npan + me_p

    def rows_of(slot, first, size):
        return pl.ds(pl.multiple_of(slot * chunk + first, 16), size)

    def cols(first, size):
        return pl.ds(pl.multiple_of(first, 128), size)

    def for_peers(do):
        def step(j, carry):
            side, p = j // npan, lax.rem(j, npan)
            other = me_b + side - 1
            ok = (other >= 0) & (other < nbub) & jnp.logical_not((side == 1) & (p == me_p))

            @pl.when(ok)
            def _():
                do(j, side, p, other)

            return carry

        lax.fori_loop(0, peers, step, 0)

    def for_others(count, me, do):
        def step(j, carry):
            @pl.when(j != me)
            def _():
                do(j)

            return carry

        lax.fori_loop(0, count, step, 0)

    barrier = pltpu.get_barrier_semaphore()

    def greet(j, side, p, other):
        pl.semaphore_signal(barrier, inc=1, device_id=(other, p), device_id_type=MESH)

    def greet_bubble(j):
        pl.semaphore_signal(barrier, inc=1, device_id=(j, me_p), device_id_type=MESH)

    for_peers(greet)
    for_others(nbub, me_b, greet_bubble)

    mom_copy = pltpu.make_async_copy(mom_hbm, mom_v, map_sem.at[0])
    spread_copy = pltpu.make_async_copy(spread_hbm, spread_v, map_sem.at[1])
    mom_copy.start()

    def near_copy(q):
        two = pl.ds(2 * q, 2)
        return pltpu.make_async_copy(near_hbm.at[:, two], near_v.at[:, two], near_sem.at[q])

    def inv_copy(q):
        two = pl.ds(2 * q, 2)
        return pltpu.make_async_copy(inv_hbm.at[:, two], inv_v.at[:, two], inv_sem.at[q])

    def start_load(q, carry):
        near_copy(q).start()
        inv_copy(q).start()
        return carry

    lax.fori_loop(0, 1, start_load, 0)
    spread_copy.start()
    lax.fori_loop(1, pairs, start_load, 0)

    def place(q, carry):
        both = jnp.concatenate(
            [dens_ref[:, cols(2 * q * blk, blk)], dens_ref[:, cols((2 * q + 1) * blk, blk)]], axis=0
        )
        hood[0, rows_of(own_slot, q * 16, 16), :] = both.astype(BF16)
        return carry

    lax.fori_loop(0, pairs, place, 0)

    @pl.when(me_b == 0)
    def _():
        hood[:, pl.ds(0, npan * chunk), :] = jnp.zeros((2, npan * chunk, blk), BF16)

    @pl.when(me_b == nbub - 1)
    def _():
        hood[:, pl.ds(2 * npan * chunk, npan * chunk), :] = jnp.zeros((2, npan * chunk, blk), BF16)

    sides = (me_b > 0).astype(jnp.int32) + (me_b < nbub - 1).astype(jnp.int32)
    pl.semaphore_wait(barrier, npan - 1 + npan * sides + nbub - 1)

    def dens_copy(sem, phase, first, size, j, side, p, other):
        piece = hood.at[phase, rows_of(own_slot, first, size)]
        back = (2 - side) * npan + me_p
        return pltpu.make_async_remote_copy(
            src_ref=piece,
            dst_ref=hood.at[phase, rows_of(back, first, size)],
            send_sem=dens_send.at[sem, j],
            recv_sem=dens_recv.at[sem, back],
            device_id=(other, p),
            device_id_type=MESH,
        )

    def dens_arrival(sem, phase, first, size, j, side, p, other):
        piece = hood.at[phase, rows_of(j, first, size)]
        return pltpu.make_async_remote_copy(
            src_ref=piece,
            dst_ref=piece,
            send_sem=dens_send.at[sem, j],
            recv_sem=dens_recv.at[sem, j],
            device_id=(other, p),
            device_id_type=MESH,
        )

    def part_copy(phase, slot, p):
        return pltpu.make_async_remote_copy(
            src_ref=part_mom.at[phase, me_p],
            dst_ref=part_mom.at[phase, slot],
            send_sem=part_send.at[phase, p],
            recv_sem=part_recv.at[phase, slot],
            device_id=(me_b, p),
            device_id_type=MESH,
        )

    def mom_copy_to(phase, slot, b):
        return pltpu.make_async_remote_copy(
            src_ref=all_mom.at[phase, me_b],
            dst_ref=all_mom.at[phase, slot],
            send_sem=mom_send.at[phase, b],
            recv_sem=mom_recv.at[phase, slot],
            device_id=(b, me_p),
            device_id_type=MESH,
        )

    group_rows = group_pairs * 16
    pieces = [(0, 0, 0, chunk)] + [(1 + g, 1, g * group_rows, group_rows) for g in range(groups)]

    for_peers(lambda *a: dens_copy(*pieces[0], *a).start())

    lane = lax.broadcasted_iota(jnp.int32, (bub, lanes), 1)
    row = lax.broadcasted_iota(jnp.int32, (bub, lanes), 0)
    diagonal = lane // moments == row

    def send_moments(phase, source):
        partial = jnp.where(diagonal, dot_nt(source[...].astype(BF16), mom_v[...]), 0.0)
        total = jnp.sum(partial, axis=0, keepdims=True)
        part_mom[phase, me_p] = jnp.broadcast_to(total, (bub, lanes))
        for_others(npan, me_p, lambda p: part_copy(phase, me_p, p).start())

    def pass_moments(phase):
        for_others(npan, me_p, lambda p: part_copy(phase, p, p).wait_recv())
        total = part_mom[phase, 0]
        for p in range(1, npan):
            total = total + part_mom[phase, p]
        all_mom[phase, me_b] = total
        for_others(nbub, me_b, lambda b: mom_copy_to(phase, me_b, b).start())

    def far_field(phase):
        for_others(nbub, me_b, lambda b: mom_copy_to(phase, b, b).wait_recv())
        total = green[0] * all_mom[phase, 0]
        for b in range(1, nbub):
            total = total + green[b] * all_mom[phase, b]
        shift = moments
        while shift < lanes:
            total = total + pltpu.roll(total, shift, 1)
            shift *= 2
        coeff = jnp.where(diagonal, total, 0.0).astype(BF16)
        far_v[...] = jnp.dot(coeff, spread_v[...], preferred_element_type=F32)

    mom_copy.wait()
    send_moments(0, dens_ref)

    def build(b, carry):
        on = lax.broadcasted_iota(jnp.int32, (rows, rows), 0) == lax.broadcasted_iota(
            jnp.int32, (rows, rows), 1
        )
        near_bub = src_bubble_ref[b] - (me_b * bub - bub)
        block = src_block_ref[b]
        index = (near_bub // bub * npan + block // rows) * chunk
        index = index + lax.rem(block, rows) * bub + lax.rem(near_bub, bub)
        slot = lax.broadcasted_iota(jnp.int32, (slots, rows), 0)
        index = jnp.where(slot < count_ref[pl.ds(b, 1), :], index, -1).astype(F32)
        wide = jnp.concatenate(
            [
                jnp.sum(
                    jnp.where(on, jnp.broadcast_to(index[s : s + 1, :], (rows, rows)), 0.0),
                    axis=1,
                    keepdims=True,
                )
                for s in range(slots)
            ],
            axis=0,
        )
        wide = jnp.broadcast_to(wide, (slots * rows, 128))
        place_of = lax.broadcasted_iota(jnp.int32, (slots * rows, 128), 1).astype(F32)
        mine_rows = pl.ds(pl.multiple_of(b * slots * rows, 16), slots * rows)
        for c in range(peers * chunk // 128):
            hit = wide == place_of + float(c * 128)
            onehot[mine_rows, c * 128 : (c + 1) * 128] = jnp.where(hit, 1.0, 0.0).astype(BF16)
        return carry

    lax.fori_loop(0, bub, build, 0)

    which = lax.broadcasted_iota(jnp.int32, (bub, nbub * bub), 1)
    mine = which == me_b * bub + lax.broadcasted_iota(jnp.int32, (bub, nbub * bub), 0)
    own = [
        jnp.sum(jnp.where(mine, centres_ref[c : c + 1, :], 0.0), axis=1, keepdims=True)
        for c in range(3)
    ]
    spot = lax.broadcasted_iota(jnp.int32, (nbub * bub, lanes), 0)
    over = lax.broadcasted_iota(jnp.int32, (nbub * bub, lanes), 1) // moments
    for b in range(nbub):
        spread_out = jnp.where(spot == over + b * bub, 1.0, 0.0)
        wide = jnp.dot(
            centres_ref[...], spread_out, precision=lax.Precision.HIGHEST, preferred_element_type=F32
        )
        dx, dy, dz = [own[c] - wide[c : c + 1, :] for c in range(3)]
        flat = dx * dx + dy * dy
        up = own[2] + wide[2:3, :]
        value = 1.0 / jnp.sqrt(flat + dz * dz + 1.0) + 1.0 / jnp.sqrt(flat + up * up + 1.0)
        gap = jnp.abs(me_b * bub + row - (b * bub + lane // moments))
        green[b] = jnp.where(gap > bub, value, 0.0)

    tint = jnp.zeros((bub, blk), jnp.int32)
    line = lax.broadcasted_iota(jnp.int32, (bub, blk), 0)
    for b in range(bub):
        tint = jnp.where(line == b, colour_ref[b], tint)

    pass_moments(0)

    def pick(phase):
        size = slots * rows
        half = bub // 2

        def step(h, carry):
            some = onehot[pl.ds(pl.multiple_of(h * half * size, 16), half * size), :]
            got = jnp.dot(some, hood[phase], preferred_element_type=F32)
            for o in range(half):
                picked[pl.ds(h * half + o, size, stride=bub), :] = got[o * size : (o + 1) * size]
            return carry

        lax.fori_loop(0, 2, step, 0)

    line_two = lax.rem(lax.broadcasted_iota(jnp.int32, (2 * bub, blk), 0), bub)

    def by_bubble(parts, right_of, count):
        total = None
        for first in range(0, bub, count):
            some = range(first, first + count)
            left = jnp.concatenate(
                [jnp.where(line_two == b, part, 0.0) for b in some for part in parts], axis=1
            )
            right = jnp.concatenate([right_of(b) for b in some], axis=1)
            got = dot_nt(left.astype(BF16), right)
            total = got if total is None else total + got
        return jnp.concatenate([total[:bub, :blk], total[bub:, blk:]], axis=0)

    def stacked(ref, q):
        first, second = cols(2 * q * blk, blk), cols((2 * q + 1) * blk, blk)
        return jnp.concatenate([ref[:, first], ref[:, second]], axis=0)

    ones = jnp.ones((2 * bub, blk), F32)

    def near_block(b, q):
        both = []
        for o in range(2):
            terms = []
            for s in range(slots):
                at = (s * rows + 2 * q + o) * bub + b
                source = jnp.broadcast_to(picked[pl.ds(at, 1), :], (16, blk)).astype(BF16)
                blocks = near_v[b, 2 * q + o, s].reshape(blk // 16, 16, blk)
                terms.append(blocks * source[None])
            while len(terms) > 1:
                terms = [sum(terms[i + 1 : i + 2], terms[i]) for i in range(0, len(terms), 2)]
            both.append(terms[0].reshape(blk, blk))
        return jnp.concatenate(both, axis=0)

    def inv_block(b, q):
        return jnp.concatenate([inv_v[b, 2 * q], inv_v[b, 2 * q + 1]], axis=0)

    both_tint = jnp.concatenate([tint, tint], axis=0)

    def solve(phase, old_ref, some):
        rests = []
        for q in some:
            near = by_bubble([ones], lambda b: near_block(b, q), 2)
            rests.append(stacked(rhs_ref, q) - near - stacked(far_v, q))
        news = []
        for q, rest in zip(some, rests):
            updated = by_bubble([rest], lambda b: inv_block(b, q), bub)
            news.append(jnp.where(both_tint == phase, updated, stacked(old_ref, q)))
        for q, new in zip(some, news):
            out_ref[:, cols(2 * q * blk, blk)] = new[:bub]
            out_ref[:, cols((2 * q + 1) * blk, blk)] = new[bub:]
        return news

    spread_copy.wait()
    for_peers(lambda *a: dens_arrival(*pieces[0], *a).wait_recv())
    pick(0)
    far_field(0)
    batch = 2 if group_pairs % 2 == 0 else 1

    def first_colour(t, carry):
        some = [batch * t + o for o in range(batch)]
        for q in some:
            near_copy(q).wait()
            inv_copy(q).wait()
        for q, new in zip(some, solve(0, dens_ref, some)):
            hood[1, rows_of(own_slot, q * 16, 16), :] = new.astype(BF16)
        return carry

    steps = group_pairs // batch
    for g in range(groups):
        lax.fori_loop(g * steps, (g + 1) * steps, first_colour, 0)
        for_peers(lambda *a: dens_copy(*pieces[1 + g], *a).start())

    send_moments(1, out_ref)
    pass_moments(1)
    for g in range(groups):
        for_peers(lambda *a: dens_arrival(*pieces[1 + g], *a).wait_recv())
    pick(1)
    far_field(1)

    def second_colour(t, carry):
        solve(1, out_ref, [batch * t + o for o in range(batch)])
        return carry

    lax.fori_loop(0, pairs // batch, second_colour, 0)

    for piece in pieces:
        for_peers(lambda *a: dens_copy(*piece, *a).wait_send())
    for phase in range(2):
        for_others(npan, me_p, lambda p: part_copy(phase, me_p, p).wait_send())
        for_others(nbub, me_b, lambda b: mom_copy_to(phase, me_b, b).wait_send())


def per_device(
    density,
    right_side,
    inv_diag,
    near_vals,
    near_bubble,
    near_block,
    near_count,
    colour,
    moment_map,
    spread_map,
    centres,
):
    nbub, npan = lax.axis_size("bubble"), lax.axis_size("panel")
    bub, panels = density.shape
    rows, slots, blk = near_vals.shape[1:4]
    moments = moment_map.shape[1]
    lanes = bub * moments
    groups = 3 if (rows // 2) % 3 == 0 else 1
    pairs = rows // 2
    chunk = rows * bub
    hood_rows = 3 * npan * chunk
    vmem = pl.BlockSpec(memory_space=pltpu.VMEM)
    smem = pl.BlockSpec(memory_space=pltpu.SMEM)
    hbm = pl.BlockSpec(memory_space=pl.ANY)
    dma = pltpu.SemaphoreType.DMA
    return pl.pallas_call(
        functools.partial(kernel, nbub, npan, groups),
        out_shape=jax.ShapeDtypeStruct(density.shape, F32),
        in_specs=[vmem, vmem, hbm, hbm, vmem, vmem, vmem, smem, hbm, hbm, vmem],
        out_specs=vmem,
        scratch_shapes=[
            pltpu.VMEM(near_vals.shape, BF16),
            pltpu.VMEM(inv_diag.shape, BF16),
            pltpu.VMEM((lanes, panels), BF16),
            pltpu.VMEM((lanes, panels), BF16),
            pltpu.VMEM((2, hood_rows, blk), BF16),
            pltpu.VMEM((bub * slots * rows, hood_rows), BF16),
            pltpu.VMEM((slots * rows * bub, blk), F32),
            pltpu.VMEM((2, npan, bub, lanes), F32),
            pltpu.VMEM((2, nbub, bub, lanes), F32),
            pltpu.VMEM((nbub, bub, lanes), F32),
            pltpu.VMEM((bub, panels), F32),
            dma((pairs,)),
            dma((pairs,)),
            dma((2,)),
            dma((1 + groups, 3 * npan)),
            dma((1 + groups, 3 * npan)),
            dma((2, npan)),
            dma((2, npan)),
            dma((2, nbub)),
            dma((2, nbub)),
        ],
        compiler_params=pltpu.CompilerParams(
            collective_id=0, has_side_effects=True, vmem_limit_bytes=56 * 1024 * 1024
        ),
    )(
        density,
        right_side,
        inv_diag,
        near_vals,
        near_bubble.transpose(0, 2, 1),
        near_block.transpose(0, 2, 1),
        near_count,
        colour,
        moment_map.reshape(lanes, panels),
        spread_map.reshape(lanes, panels),
        centres,
    )


def solution(mesh):
    in_specs = (
        P("bubble", "panel"),
        P("bubble", "panel"),
        P("bubble", "panel", None, None),
        P("bubble", "panel", None, None, None),
        P("bubble", "panel", None),
        P("bubble", "panel", None),
        P("bubble", "panel"),
        P("bubble"),
        P("bubble", None, "panel"),
        P("bubble", None, "panel"),
        P(),
    )
    out_specs = P("bubble", "panel")
    return jax.shard_map(
        per_device, mesh=mesh, in_specs=in_specs, out_specs=out_specs, check_vma=False
    )
```

```python
import functools

import jax
import jax.numpy as jnp
from jax import lax
from jax.experimental import pallas as pl
from jax.experimental.pallas import tpu as pltpu
from jax.sharding import PartitionSpec as P

MESH = pl.DeviceIdType.MESH
F32 = jnp.float32
BF16 = jnp.bfloat16


def dot_nt(left, right):
    return lax.dot_general(left, right, (((1,), (1,)), ((), ())), preferred_element_type=F32)


def kernel(
    nbub,
    npan,
    groups,
    dens_ref,
    rhs_ref,
    inv_hbm,
    near_hbm,
    src_bubble_ref,
    src_block_ref,
    count_ref,
    colour_ref,
    mom_hbm,
    spread_hbm,
    centres_ref,
    out_ref,
    near_v,
    inv_v,
    mom_v,
    spread_v,
    hood,
    onehot,
    picked,
    part_mom,
    all_mom,
    green,
    far_v,
    near_sem,
    inv_sem,
    map_sem,
    dens_send,
    dens_recv,
    part_send,
    part_recv,
    mom_send,
    mom_recv,
):
    bub, panels = dens_ref.shape
    rows, slots, blk = near_v.shape[1], near_v.shape[2], near_v.shape[3]
    pairs = rows // 2
    chunk = rows * bub
    moments = mom_v.shape[0] // bub
    lanes = bub * moments
    peers = 3 * npan
    group_pairs = pairs // groups
    me_b, me_p = lax.axis_index("bubble"), lax.axis_index("panel")
    own_slot = npan + me_p

    def rows_of(slot, first, size):
        return pl.ds(pl.multiple_of(slot * chunk + first, 16), size)

    def cols(first, size):
        return pl.ds(pl.multiple_of(first, 128), size)

    def for_peers(do):
        def step(j, carry):
            side, p = j // npan, lax.rem(j, npan)
            other = me_b + side - 1
            ok = (other >= 0) & (other < nbub) & jnp.logical_not((side == 1) & (p == me_p))

            @pl.when(ok)
            def _():
                do(j, side, p, other)

            return carry

        lax.fori_loop(0, peers, step, 0)

    def for_others(count, me, do):
        def step(j, carry):
            @pl.when(j != me)
            def _():
                do(j)

            return carry

        lax.fori_loop(0, count, step, 0)

    barrier = pltpu.get_barrier_semaphore()

    def greet(j, side, p, other):
        pl.semaphore_signal(barrier, inc=1, device_id=(other, p), device_id_type=MESH)

    def greet_bubble(j):
        pl.semaphore_signal(barrier, inc=1, device_id=(j, me_p), device_id_type=MESH)

    for_peers(greet)
    for_others(nbub, me_b, greet_bubble)

    mom_copy = pltpu.make_async_copy(mom_hbm, mom_v, map_sem.at[0])
    spread_copy = pltpu.make_async_copy(spread_hbm, spread_v, map_sem.at[1])
    mom_copy.start()

    def near_copy(q):
        two = pl.ds(2 * q, 2)
        return pltpu.make_async_copy(near_hbm.at[:, two], near_v.at[:, two], near_sem.at[q])

    def inv_copy(q):
        two = pl.ds(2 * q, 2)
        return pltpu.make_async_copy(inv_hbm.at[:, two], inv_v.at[:, two], inv_sem.at[q])

    def start_load(q, carry):
        near_copy(q).start()
        inv_copy(q).start()
        return carry

    lax.fori_loop(0, 1, start_load, 0)
    spread_copy.start()
    lax.fori_loop(1, pairs, start_load, 0)

    def place(q, carry):
        both = jnp.concatenate(
            [dens_ref[:, cols(2 * q * blk, blk)], dens_ref[:, cols((2 * q + 1) * blk, blk)]], axis=0
        )
        hood[0, rows_of(own_slot, q * 16, 16), :] = both.astype(BF16)
        return carry

    lax.fori_loop(0, pairs, place, 0)

    @pl.when(me_b == 0)
    def _():
        hood[:, pl.ds(0, npan * chunk), :] = jnp.zeros((2, npan * chunk, blk), BF16)

    @pl.when(me_b == nbub - 1)
    def _():
        hood[:, pl.ds(2 * npan * chunk, npan * chunk), :] = jnp.zeros((2, npan * chunk, blk), BF16)

    sides = (me_b > 0).astype(jnp.int32) + (me_b < nbub - 1).astype(jnp.int32)
    pl.semaphore_wait(barrier, npan - 1 + npan * sides + nbub - 1)

    def dens_copy(sem, phase, first, size, j, side, p, other):
        piece = hood.at[phase, rows_of(own_slot, first, size)]
        back = (2 - side) * npan + me_p
        return pltpu.make_async_remote_copy(
            src_ref=piece,
            dst_ref=hood.at[phase, rows_of(back, first, size)],
            send_sem=dens_send.at[sem, j],
            recv_sem=dens_recv.at[sem, back],
            device_id=(other, p),
            device_id_type=MESH,
        )

    def dens_arrival(sem, phase, first, size, j, side, p, other):
        piece = hood.at[phase, rows_of(j, first, size)]
        return pltpu.make_async_remote_copy(
            src_ref=piece,
            dst_ref=piece,
            send_sem=dens_send.at[sem, j],
            recv_sem=dens_recv.at[sem, j],
            device_id=(other, p),
            device_id_type=MESH,
        )

    def part_copy(phase, slot, p):
        return pltpu.make_async_remote_copy(
            src_ref=part_mom.at[phase, me_p],
            dst_ref=part_mom.at[phase, slot],
            send_sem=part_send.at[phase, p],
            recv_sem=part_recv.at[phase, slot],
            device_id=(me_b, p),
            device_id_type=MESH,
        )

    def mom_copy_to(phase, slot, b):
        return pltpu.make_async_remote_copy(
            src_ref=all_mom.at[phase, me_b],
            dst_ref=all_mom.at[phase, slot],
            send_sem=mom_send.at[phase, b],
            recv_sem=mom_recv.at[phase, slot],
            device_id=(b, me_p),
            device_id_type=MESH,
        )

    group_rows = group_pairs * 16
    pieces = [(0, 0, 0, chunk)] + [(1 + g, 1, g * group_rows, group_rows) for g in range(groups)]

    for_peers(lambda *a: dens_copy(*pieces[0], *a).start())

    lane = lax.broadcasted_iota(jnp.int32, (bub, lanes), 1)
    row = lax.broadcasted_iota(jnp.int32, (bub, lanes), 0)
    diagonal = lane // moments == row

    def send_moments(phase, source):
        partial = jnp.where(diagonal, dot_nt(source[...].astype(BF16), mom_v[...]), 0.0)
        total = jnp.sum(partial, axis=0, keepdims=True)
        part_mom[phase, me_p] = jnp.broadcast_to(total, (bub, lanes))
        for_others(npan, me_p, lambda p: part_copy(phase, me_p, p).start())

    def pass_moments(phase):
        for_others(npan, me_p, lambda p: part_copy(phase, p, p).wait_recv())
        total = part_mom[phase, 0]
        for p in range(1, npan):
            total = total + part_mom[phase, p]
        all_mom[phase, me_b] = total
        for_others(nbub, me_b, lambda b: mom_copy_to(phase, me_b, b).start())

    def far_field(phase):
        for_others(nbub, me_b, lambda b: mom_copy_to(phase, b, b).wait_recv())
        total = green[0] * all_mom[phase, 0]
        for b in range(1, nbub):
            total = total + green[b] * all_mom[phase, b]
        shift = moments
        while shift < lanes:
            total = total + pltpu.roll(total, shift, 1)
            shift *= 2
        coeff = jnp.where(diagonal, total, 0.0).astype(BF16)
        far_v[...] = jnp.dot(coeff, spread_v[...], preferred_element_type=F32)

    mom_copy.wait()
    send_moments(0, dens_ref)

    def build(b, carry):
        on = lax.broadcasted_iota(jnp.int32, (rows, rows), 0) == lax.broadcasted_iota(
            jnp.int32, (rows, rows), 1
        )
        near_bub = src_bubble_ref[b] - (me_b * bub - bub)
        block = src_block_ref[b]
        index = (near_bub // bub * npan + block // rows) * chunk
        index = index + lax.rem(block, rows) * bub + lax.rem(near_bub, bub)
        slot = lax.broadcasted_iota(jnp.int32, (slots, rows), 0)
        index = jnp.where(slot < count_ref[pl.ds(b, 1), :], index, -1).astype(F32)
        wide = jnp.concatenate(
            [
                jnp.sum(
                    jnp.where(on, jnp.broadcast_to(index[s : s + 1, :], (rows, rows)), 0.0),
                    axis=1,
                    keepdims=True,
                )
                for s in range(slots)
            ],
            axis=0,
        )
        wide = jnp.broadcast_to(wide, (slots * rows, 128))
        place_of = lax.broadcasted_iota(jnp.int32, (slots * rows, 128), 1).astype(F32)
        mine_rows = pl.ds(pl.multiple_of(b * slots * rows, 16), slots * rows)
        for c in range(peers * chunk // 128):
            hit = wide == place_of + float(c * 128)
            onehot[mine_rows, c * 128 : (c + 1) * 128] = jnp.where(hit, 1.0, 0.0).astype(BF16)
        return carry

    lax.fori_loop(0, bub, build, 0)

    which = lax.broadcasted_iota(jnp.int32, (bub, nbub * bub), 1)
    mine = which == me_b * bub + lax.broadcasted_iota(jnp.int32, (bub, nbub * bub), 0)
    own = [
        jnp.sum(jnp.where(mine, centres_ref[c : c + 1, :], 0.0), axis=1, keepdims=True)
        for c in range(3)
    ]
    spot = lax.broadcasted_iota(jnp.int32, (nbub * bub, lanes), 0)
    over = lax.broadcasted_iota(jnp.int32, (nbub * bub, lanes), 1) // moments
    for b in range(nbub):
        spread_out = jnp.where(spot == over + b * bub, 1.0, 0.0)
        wide = jnp.dot(
            centres_ref[...], spread_out, precision=lax.Precision.HIGHEST, preferred_element_type=F32
        )
        dx, dy, dz = [own[c] - wide[c : c + 1, :] for c in range(3)]
        flat = dx * dx + dy * dy
        up = own[2] + wide[2:3, :]
        value = 1.0 / jnp.sqrt(flat + dz * dz + 1.0) + 1.0 / jnp.sqrt(flat + up * up + 1.0)
        gap = jnp.abs(me_b * bub + row - (b * bub + lane // moments))
        green[b] = jnp.where(gap > bub, value, 0.0)

    tint = jnp.zeros((bub, blk), jnp.int32)
    line = lax.broadcasted_iota(jnp.int32, (bub, blk), 0)
    for b in range(bub):
        tint = jnp.where(line == b, colour_ref[b], tint)

    pass_moments(0)

    def pick(phase):
        size = slots * rows
        half = bub // 2

        def step(h, carry):
            some = onehot[pl.ds(pl.multiple_of(h * half * size, 16), half * size), :]
            got = jnp.dot(some, hood[phase], preferred_element_type=F32)
            for o in range(half):
                picked[pl.ds(h * half + o, size, stride=bub), :] = got[o * size : (o + 1) * size]
            return carry

        lax.fori_loop(0, 2, step, 0)

    line_two = lax.rem(lax.broadcasted_iota(jnp.int32, (2 * bub, blk), 0), bub)

    def by_bubble(parts, right_of, count):
        total = None
        for first in range(0, bub, count):
            some = range(first, first + count)
            left = jnp.concatenate(
                [jnp.where(line_two == b, part, 0.0) for b in some for part in parts], axis=1
            )
            right = jnp.concatenate([right_of(b) for b in some], axis=1)
            got = dot_nt(left.astype(BF16), right)
            total = got if total is None else total + got
        return jnp.concatenate([total[:bub, :blk], total[bub:, blk:]], axis=0)

    def stacked(ref, q):
        first, second = cols(2 * q * blk, blk), cols((2 * q + 1) * blk, blk)
        return jnp.concatenate([ref[:, first], ref[:, second]], axis=0)

    ones = jnp.ones((2 * bub, blk), F32)

    def near_block(b, q):
        both = []
        for o in range(2):
            terms = []
            for s in range(slots):
                at = (s * rows + 2 * q + o) * bub + b
                source = jnp.broadcast_to(picked[pl.ds(at, 1), :], (16, blk)).astype(BF16)
                blocks = near_v[b, 2 * q + o, s].reshape(blk // 16, 16, blk)
                terms.append(blocks * source[None])
            terms = [sum(terms[i + 1 : i + 2], terms[i]) for i in range(0, slots, 2)]
            both.append(jnp.concatenate([term.reshape(blk, blk) for term in terms], axis=1))
        return jnp.concatenate(both, axis=0)

    def inv_block(b, q):
        return jnp.concatenate([inv_v[b, 2 * q], inv_v[b, 2 * q + 1]], axis=0)

    both_tint = jnp.concatenate([tint, tint], axis=0)

    def solve(phase, old_ref, some):
        rests = []
        for q in some:
            near = by_bubble([ones] * ((slots + 1) // 2), lambda b: near_block(b, q), 1)
            rests.append(stacked(rhs_ref, q) - near - stacked(far_v, q))
        news = []
        for q, rest in zip(some, rests):
            updated = by_bubble([rest], lambda b: inv_block(b, q), bub)
            news.append(jnp.where(both_tint == phase, updated, stacked(old_ref, q)))
        for q, new in zip(some, news):
            out_ref[:, cols(2 * q * blk, blk)] = new[:bub]
            out_ref[:, cols((2 * q + 1) * blk, blk)] = new[bub:]
        return news

    spread_copy.wait()
    for_peers(lambda *a: dens_arrival(*pieces[0], *a).wait_recv())
    pick(0)
    far_field(0)
    batch = 4 if group_pairs % 4 == 0 else 1

    def first_colour(t, carry):
        some = [batch * t + o for o in range(batch)]
        for q in some:
            near_copy(q).wait()
            inv_copy(q).wait()
        for q, new in zip(some, solve(0, dens_ref, some)):
            hood[1, rows_of(own_slot, q * 16, 16), :] = new.astype(BF16)
        return carry

    steps = group_pairs // batch
    for g in range(groups):
        lax.fori_loop(g * steps, (g + 1) * steps, first_colour, 0)
        for_peers(lambda *a: dens_copy(*pieces[1 + g], *a).start())

    send_moments(1, out_ref)
    pass_moments(1)
    for g in range(groups):
        for_peers(lambda *a: dens_arrival(*pieces[1 + g], *a).wait_recv())
    pick(1)
    far_field(1)

    def second_colour(t, carry):
        solve(1, out_ref, [batch * t + o for o in range(batch)])
        return carry

    lax.fori_loop(0, pairs // batch, second_colour, 0)

    for piece in pieces:
        for_peers(lambda *a: dens_copy(*piece, *a).wait_send())
    for phase in range(2):
        for_others(npan, me_p, lambda p: part_copy(phase, me_p, p).wait_send())
        for_others(nbub, me_b, lambda b: mom_copy_to(phase, me_b, b).wait_send())


def per_device(
    density,
    right_side,
    inv_diag,
    near_vals,
    near_bubble,
    near_block,
    near_count,
    colour,
    moment_map,
    spread_map,
    centres,
):
    nbub, npan = lax.axis_size("bubble"), lax.axis_size("panel")
    bub, panels = density.shape
    rows, slots, blk = near_vals.shape[1:4]
    moments = moment_map.shape[1]
    lanes = bub * moments
    groups = 3 if (rows // 2) % 3 == 0 else 1
    pairs = rows // 2
    chunk = rows * bub
    hood_rows = 3 * npan * chunk
    vmem = pl.BlockSpec(memory_space=pltpu.VMEM)
    smem = pl.BlockSpec(memory_space=pltpu.SMEM)
    hbm = pl.BlockSpec(memory_space=pl.ANY)
    dma = pltpu.SemaphoreType.DMA
    return pl.pallas_call(
        functools.partial(kernel, nbub, npan, groups),
        out_shape=jax.ShapeDtypeStruct(density.shape, F32),
        in_specs=[vmem, vmem, hbm, hbm, vmem, vmem, vmem, smem, hbm, hbm, vmem],
        out_specs=vmem,
        scratch_shapes=[
            pltpu.VMEM(near_vals.shape, BF16),
            pltpu.VMEM(inv_diag.shape, BF16),
            pltpu.VMEM((lanes, panels), BF16),
            pltpu.VMEM((lanes, panels), BF16),
            pltpu.VMEM((2, hood_rows, blk), BF16),
            pltpu.VMEM((bub * slots * rows, hood_rows), BF16),
            pltpu.VMEM((slots * rows * bub, blk), F32),
            pltpu.VMEM((2, npan, bub, lanes), F32),
            pltpu.VMEM((2, nbub, bub, lanes), F32),
            pltpu.VMEM((nbub, bub, lanes), F32),
            pltpu.VMEM((bub, panels), F32),
            dma((pairs,)),
            dma((pairs,)),
            dma((2,)),
            dma((1 + groups, 3 * npan)),
            dma((1 + groups, 3 * npan)),
            dma((2, npan)),
            dma((2, npan)),
            dma((2, nbub)),
            dma((2, nbub)),
        ],
        compiler_params=pltpu.CompilerParams(
            collective_id=0, has_side_effects=True, vmem_limit_bytes=56 * 1024 * 1024
        ),
    )(
        density,
        right_side,
        inv_diag,
        near_vals,
        near_bubble.transpose(0, 2, 1),
        near_block.transpose(0, 2, 1),
        near_count,
        colour,
        moment_map.reshape(lanes, panels),
        spread_map.reshape(lanes, panels),
        centres,
    )


def solution(mesh):
    in_specs = (
        P("bubble", "panel"),
        P("bubble", "panel"),
        P("bubble", "panel", None, None),
        P("bubble", "panel", None, None, None),
        P("bubble", "panel", None),
        P("bubble", "panel", None),
        P("bubble", "panel"),
        P("bubble"),
        P("bubble", None, "panel"),
        P("bubble", None, "panel"),
        P(),
    )
    out_specs = P("bubble", "panel")
    return jax.shard_map(
        per_device, mesh=mesh, in_specs=in_specs, out_specs=out_specs, check_vma=False
    )
```
